32 devices in a mesh: row: 16 (over z, y, core), col: 2 (over x).
Axes of the slice: x: 2, y: 2, z: 4, core: 2. Of those that a mesh axis runs over, the one named last changes fastest.
Arguments:
- left_slots: float32 [16, 1024, 512], P('row', 'col'), may hold values from -0.15625 to 0.15625
- right: float32 [2048, 4096], P('col', 'row'), may hold values from -6 to 6
- previous: float32 [1024, 4096], P('col', 'row'), may hold values from -4 to 4
- offsets: int32 [3], replicated, may hold values from 0 to 3, as said below
- owners: int32 [2, 3], P('col'), may hold values from 0 to 15, as said below
Outputs:
- next_density: float32 [1024, 4096], P('col', 'row')
The draws below stay inside these ranges and needn't reach their ends.
Inputs may be any that keep to these rules, and one draw needn't show every extreme that they name: `offsets`: distinct, in any order; they include 0 and 3. `owners`: distinct within each grid row.
All inputs are finite; a program needn't handle non-finite values.
Results may differ from the reference program's by a relative error of at most 0.0001.
Values sent between devices are 32-bit elements; how exact they have to be, the bound alone decides.
No kernel may reach another device: no remote copies, remote signals or barrier semaphores. Data moves between devices by JAX's collectives and lax.ppermute only.
A program may use at most 64 MiB of HBM per device.

```python
import jax
import jax.numpy as jnp
from jax import lax

KW = 512
KB_PER = 2
ROWS_DEV = 512
KBL = 4
NDIAG = 3
KDIM = 2048
ROWS = 1024
COLS = 4096
N_ROW = 16
N_COL = 2


def draw_offsets(key, part):
    inner = jax.random.permutation(jax.random.fold_in(key, 11), KBL - 2) + 1
    chosen = jnp.concatenate([jnp.zeros((1,), jnp.int32), inner[:NDIAG - 2].astype(jnp.int32), jnp.full((1,), KBL - 1, jnp.int32)])
    order = jax.random.permutation(jax.random.fold_in(key, 37), NDIAG)
    return chosen[order].astype(jnp.int32)


def draw_owners(key, part):
    used = min(N_COL * NDIAG, N_ROW)
    rest = (jax.random.permutation(jax.random.fold_in(key, 23), N_ROW - 2) + 1).astype(jnp.int32)
    order = jnp.concatenate([jnp.full((1,), N_ROW - 1, jnp.int32), jnp.zeros((1,), jnp.int32), rest])
    offset_shift = jax.random.randint(jax.random.fold_in(key, 29), (), 0, used - 1)
    order = jnp.roll(order, offset_shift)
    where_at = (jnp.arange(N_COL)[:, None] * NDIAG + jnp.arange(NDIAG)[None, :]) % N_ROW
    return order[where_at].astype(jnp.int32)


def shard_levels(key, shape, split, smallest, top_value):
    def one(position, parts):
        heights = jax.random.uniform(jax.random.fold_in(jax.random.fold_in(key, 6), position), (parts,), jnp.float32, smallest / len(split), top_value / len(split))
        return jnp.repeat(jnp.exp(heights), shape[position] // parts).reshape((-1,) + (1,) * (len(shape) - position - 1))

    factor_of = one(*split[0])
    for cut in split[1:]:
        factor_of = factor_of * one(*cut)
    return factor_of


def centred(own_key, dims, width, reach, cuts=(), dtype=jnp.bfloat16):
    array = width * jax.random.normal(own_key, dims, jnp.float32)
    if cuts:
        array = array * shard_levels(own_key, dims, cuts, -0.22, 0.18)
    return jnp.clip(array, -reach, reach).astype(dtype)


def setup_inputs(seed: int = 0) -> dict:
    key_list = jax.random.split(jax.random.key(seed), 6)
    left_slots = centred(key_list[0], (N_ROW, ROWS, KW), (NDIAG * KW) ** -0.5, 0.15625, ((0, 16), (1, 2)), jnp.float32)
    right = centred(key_list[1], (KDIM, COLS), 1.0, 6.0, ((0, 2), (1, 16)), jnp.float32)
    previous = centred(key_list[2], (ROWS, COLS), 0.5, 4.0, ((0, 2), (1, 16)), jnp.float32)
    offsets = draw_offsets(jax.random.fold_in(key_list[5], 71), 0)
    owners = draw_owners(jax.random.fold_in(key_list[5], 71), 0)
    return {"left_slots": left_slots, "right": right, "previous": previous, "offsets": offsets, "owners": owners}


def reference(left_slots, right, previous, offsets, owners):
    row_parts = []
    for grid_row in range(N_COL):
        partial_sum = jnp.zeros((ROWS_DEV, right.shape[1]), jnp.float32)
        for number in range(NDIAG):
            holder = owners[grid_row, number]
            slab = lax.dynamic_index_in_dim(left_slots, holder.astype(jnp.int32), 0, keepdims=False)
            slab = slab[grid_row * ROWS_DEV:(grid_row + 1) * ROWS_DEV, :]
            block = (KB_PER * grid_row + offsets[number]) % KBL
            piece = lax.dynamic_slice_in_dim(right, (block * KW).astype(jnp.int32), KW, 0)
            partial_sum = partial_sum + jnp.dot(slab, piece, precision=lax.Precision.HIGHEST, preferred_element_type=jnp.float32)
        row_parts.append(partial_sum)
    product = jnp.concatenate(row_parts, axis=0)
    return 2.0 * previous - product
```

```python
import functools

import jax
import jax.numpy as jnp
from jax import lax
from jax.experimental import pallas as pl
from jax.experimental.pallas import tpu as pltpu
from jax.sharding import PartitionSpec as P


def split(value):
    high = value.astype(jnp.bfloat16)
    low = (value - high.astype(jnp.float32)).astype(jnp.bfloat16)
    return high, low


def dot(left, right):
    return jnp.dot(left, right, preferred_element_type=jnp.float32)


def combine_kernel(count, group, scalars, *refs):
    parts = refs[:group]
    right_refs = refs[group:group + count]
    previous, out, high_scratch, low_scratch = refs[group + count:]
    chunk = parts[0].shape[1]
    total = 2.0 * previous[...]
    for number in range(count):
        mask = scalars[number]
        for step in range(group):
            place = pl.multiple_of((mask ^ step) * chunk, chunk)
            high, low = split(parts[step][number])
            high_scratch[number, pl.ds(place, chunk), :] = high
            low_scratch[number, pl.ds(place, chunk), :] = low
        right_high, right_low = split(right_refs[number][...])
        left_high = high_scratch[number]
        left_low = low_scratch[number]
        total = total - (dot(left_high, right_low) + dot(left_low, right_high) + dot(left_high, right_high))
    out[...] = total


def combine(scalars, parts, right_list, previous):
    count = len(right_list)
    group = len(parts)
    rows = previous.shape[0]
    width = parts[0].shape[2]
    vmem = pl.BlockSpec(memory_space=pltpu.VMEM)
    return pl.pallas_call(
        functools.partial(combine_kernel, count, group),
        out_shape=jax.ShapeDtypeStruct(previous.shape, previous.dtype),
        in_specs=[pl.BlockSpec(memory_space=pltpu.SMEM)] + [vmem] * (group + count + 1),
        out_specs=vmem,
        scratch_shapes=[
            pltpu.VMEM((count, rows, width), jnp.bfloat16),
            pltpu.VMEM((count, rows, width), jnp.bfloat16),
        ],
        compiler_params=pltpu.CompilerParams(vmem_limit_bytes=48 * 1024 * 1024),
    )(scalars, *parts, *right_list, previous)


def shards(left_slots, right, previous, offsets, owners):
    own_block = left_slots[0]
    rows, width = own_block.shape
    count = offsets.shape[0]
    devices = lax.axis_size("row")
    columns = lax.axis_size("col")
    blocks = right.shape[0] // width
    group = devices // 2
    chunk = rows // group
    index = lax.axis_index("row")
    member, half = index % group, index // group

    def swap(array, mask):
        return lax.ppermute(array, "row", [(i, i ^ mask) for i in range(devices)])

    def shift(array, distance):
        pairs = [((i + distance) % columns, i) for i in range(columns)]
        return lax.ppermute(array, "col", pairs)

    pieces = [own_block[s * chunk:(s + 1) * chunk] for s in range(group)]
    order = sorted(range(1, group), reverse=True)
    got = {0: pieces[0]}
    for s in order:
        got[s] = swap(pieces[s], s)

    rank = jnp.sum(offsets[None, :] < offsets[:, None], axis=1)
    right_list = [right[:width]]
    sorted_offsets = [jnp.sum(jnp.where(rank == k, offsets, 0)) for k in range(count)]
    sorted_owners = [jnp.sum(jnp.where(rank == k, owners[0], 0)) for k in range(count)]
    for k in range(1, count - 1):
        offset = sorted_offsets[k]
        piece = lax.dynamic_slice_in_dim(right, (offset % blocks) * width, width, 0)
        distance = 1
        while distance < columns:
            far = (offset // blocks // distance) % 2 == 1
            piece = jnp.where(far, shift(piece, distance), piece)
            distance *= 2
        right_list.append(piece)
    right_list.append(shift(right[(blocks - 1) * width:], columns - 1))

    masks = [(owner % group) ^ member for owner in sorted_owners]
    here = [owner // group == half for owner in sorted_owners]
    mine = []
    for k in range(count):
        value = got[0]
        for s in range(1, group):
            value = jnp.where(masks[k] == s, got[s], value)
        mine.append(value)
    mine = jnp.stack(mine)
    other = swap(mine, group)
    flags = jnp.stack(here)[:, None, None]
    mine = jnp.where(flags, mine, other)

    parts = {0: mine}
    for s in range(group - 2, 0, -2):
        parts[s] = swap(mine, s)
    parts[1] = swap(mine, 1)
    for s in range(group - 2, 0, -2):
        parts[s + 1] = swap(parts[s], 1)
    scalars = jnp.stack(masks).astype(jnp.int32)
    return combine(scalars, [parts[s] for s in range(group)], right_list, previous)


def solution(mesh):
    return jax.shard_map(
        shards,
        mesh=mesh,
        in_specs=(P("row", "col", None), P("col", "row"), P("col", "row"), P(), P("col", None)),
        out_specs=P("col", "row"),
        check_vma=False,
    )
```

```python
import functools

import jax
import jax.numpy as jnp
from jax import lax
from jax.experimental import pallas as pl
from jax.experimental.pallas import tpu as pltpu
from jax.sharding import PartitionSpec as P

PARTS = 1
VMEM = pl.BlockSpec(memory_space=pltpu.VMEM)
SMEM = pl.BlockSpec(memory_space=pltpu.SMEM)
PARAMS = pltpu.CompilerParams(vmem_limit_bytes=40 * 1024 * 1024)


def split(value):
    high = value.astype(jnp.bfloat16)
    low = (value - high.astype(jnp.float32)).astype(jnp.bfloat16)
    return high, low


def dot(left, right):
    return jnp.dot(left, right, preferred_element_type=jnp.float32)


def pick_kernel(group, owners, *refs):
    pieces, out = refs[:group], refs[group]
    member = lax.axis_index("row") % group
    for number in range(out.shape[0]):
        mask = (owners[0, number] % group) ^ member
        for step in range(group):

            @pl.when(mask == step)
            def _():
                out[number] = pieces[step][...]


def merge_kernel(group, owners, mine, other, out):
    half = lax.axis_index("row") // group
    for number in range(out.shape[0]):
        here = owners[0, number] // group == half

        @pl.when(here)
        def _():
            out[number] = mine[number]

        @pl.when(jnp.logical_not(here))
        def _():
            out[number] = other[number]


def multiply_kernel(group, columns, part, offsets, owners, *refs):
    pieces, refs = refs[:group], refs[group:]
    rights, refs = refs[:columns], refs[columns:]
    previous, refs = refs[0], refs[1:]
    early, refs = refs[:-5], refs[-5:]
    out, left_high, left_low, right_high, right_low = refs
    count, chunk, width = pieces[0].shape
    blocks = rights[0].shape[0] // width
    member = lax.axis_index("row") % group
    size = group * chunk
    first = part * size
    for number in range(count):
        mask = (owners[0, number] % group) ^ member
        lanes = slice(number * width, (number + 1) * width)
        for step in range(group):
            place = pl.multiple_of((mask ^ step) * chunk, chunk)
            high, low = split(pieces[step][number])
            left_high[pl.ds(place, chunk), lanes] = high
            left_low[pl.ds(place, chunk), lanes] = low
        distance = offsets[number] // blocks
        start = pl.multiple_of((offsets[number] % blocks) * width, width)
        for step in range(columns):

            @pl.when(distance == step)
            def _():
                high, low = split(rights[step][pl.ds(start, width), :])
                right_high[lanes, :] = high
                right_low[lanes, :] = low

    total = 2.0 * previous[first:first + size, :] - (
        dot(left_high[...], right_low[...])
        + dot(left_low[...], right_high[...])
        + dot(left_high[...], right_high[...])
    )
    if early:
        for number, ref in enumerate(early):
            out[number * size:(number + 1) * size, :] = ref[...]
        out[first:first + size, :] = total
    else:
        out[...] = total


def shards(left_slots, right, previous, offsets, owners):
    own_block = left_slots[0]
    rows, width = own_block.shape
    count = offsets.shape[0]
    devices = lax.axis_size("row")
    columns = lax.axis_size("col")
    group = devices // 2
    size = rows // PARTS
    chunk = size // group

    def swap(array, mask):
        return lax.ppermute(array, "row", [(i, i ^ mask) for i in range(devices)])

    def shift(array, distance):
        pairs = [((i + distance) % columns, i) for i in range(columns)]
        return lax.ppermute(array, "col", pairs)

    def pick(pieces):
        return pl.pallas_call(
            functools.partial(pick_kernel, group),
            out_shape=jax.ShapeDtypeStruct((count, chunk, width), own_block.dtype),
            in_specs=[SMEM] + [VMEM] * group,
            out_specs=VMEM,
            compiler_params=PARAMS,
        )(owners, *pieces)

    def merge(mine, other):
        return pl.pallas_call(
            functools.partial(merge_kernel, group),
            out_shape=jax.ShapeDtypeStruct(mine.shape, mine.dtype),
            in_specs=[SMEM, VMEM, VMEM],
            out_specs=VMEM,
            compiler_params=PARAMS,
        )(owners, mine, other)

    def multiply(part, pieces, rights, early):
        shape = (rows if early else size, right.shape[1])
        return pl.pallas_call(
            functools.partial(multiply_kernel, group, columns, part),
            out_shape=jax.ShapeDtypeStruct(shape, previous.dtype),
            in_specs=[SMEM, SMEM] + [VMEM] * (group + columns + 1 + len(early)),
            out_specs=VMEM,
            scratch_shapes=[
                pltpu.VMEM((size, count * width), jnp.bfloat16),
                pltpu.VMEM((size, count * width), jnp.bfloat16),
                pltpu.VMEM((count * width, right.shape[1]), jnp.bfloat16),
                pltpu.VMEM((count * width, right.shape[1]), jnp.bfloat16),
            ],
            compiler_params=PARAMS,
        )(offsets, owners, *pieces, *rights, previous, *early)

    picked = []
    for part in range(PARTS):
        pieces = [own_block[part * size + s * chunk:part * size + (s + 1) * chunk] for s in range(group)]
        for s in range(group - 1, 0, -1):
            pieces[s] = swap(pieces[s], s)
        picked.append(pick(pieces))

    rights = [right] + [shift(right, distance) for distance in range(1, columns)]

    merged = [merge(mine, swap(mine, group)) for mine in picked]

    results = []
    for part, mine in enumerate(merged):
        pieces = {0: mine}
        for s in range(group - 2, 0, -2):
            pieces[s] = swap(mine, s)
        for s in range(0, group, 2):
            pieces[s + 1] = swap(pieces[s], 1)
        early = results if part == PARTS - 1 else []
        results.append(multiply(part, [pieces[s] for s in range(group)], rights, early))
    return results[-1]


def solution(mesh):
    return jax.shard_map(
        shards,
        mesh=mesh,
        in_specs=(P("row", "col", None), P("col", "row"), P("col", "row"), P(), P("col", None)),
        out_specs=P("col", "row"),
        check_vma=False,
    )
```

```python
import functools

import jax
import jax.numpy as jnp
from jax import lax
from jax.experimental import pallas as pl
from jax.experimental.pallas import tpu as pltpu
from jax.sharding import PartitionSpec as P

PARTS = 2
VMEM = pl.BlockSpec(memory_space=pltpu.VMEM)
SMEM = pl.BlockSpec(memory_space=pltpu.SMEM)
PARAMS = pltpu.CompilerParams(vmem_limit_bytes=40 * 1024 * 1024)


def split(value):
    high = value.astype(jnp.bfloat16)
    low = (value - high.astype(jnp.float32)).astype(jnp.bfloat16)
    return high, low


def dot(left, right):
    return jnp.dot(left, right, preferred_element_type=jnp.float32)


def pick_kernel(group, owners, *refs):
    pieces, (keep, give) = refs[:-2], refs[-2:]
    half = keep.shape[1]
    member = lax.axis_index("row") % group
    for number in range(keep.shape[0]):
        mask = ((owners[0, number] % group) ^ member) // 2
        for step, piece in enumerate(pieces):

            @pl.when(mask == step)
            def _():
                keep[number] = piece[:half, :]
                give[number] = piece[half:, :]


def merge_kernel(low, high, owners, mine, other, out):
    side = lax.axis_index("row") % high // low
    for number in range(out.shape[0]):
        here = owners[0, number] % high // low == side

        @pl.when(here)
        def _():
            out[number] = mine[number]

        @pl.when(jnp.logical_not(here))
        def _():
            out[number] = other[number]


def multiply_kernel(group, columns, part, offsets, owners, *refs):
    pieces, refs = refs[:group], refs[group:]
    rights, refs = refs[:columns], refs[columns:]
    previous, refs = refs[0], refs[1:]
    early, refs = refs[:-5], refs[-5:]
    out, left_high, left_low, right_high, right_low = refs
    count, chunk, width = pieces[0].shape
    blocks = rights[0].shape[0] // width
    member = lax.axis_index("row") % group
    size = group * chunk
    first = part * size
    for number in range(count):
        mask = (owners[0, number] % group) ^ member
        lanes = slice(number * width, (number + 1) * width)
        for step in range(group):
            place = pl.multiple_of((mask ^ step) * chunk, chunk)
            high, low = split(pieces[step][number])
            left_high[pl.ds(place, chunk), lanes] = high
            left_low[pl.ds(place, chunk), lanes] = low
        distance = offsets[number] // blocks
        start = pl.multiple_of((offsets[number] % blocks) * width, width)
        for step in range(columns):

            @pl.when(distance == step)
            def _():
                high, low = split(rights[step][pl.ds(start, width), :])
                right_high[lanes, :] = high
                right_low[lanes, :] = low

    total = 2.0 * previous[first:first + size, :] - (
        dot(left_high[...], right_low[...])
        + dot(left_low[...], right_high[...])
        + dot(left_high[...], right_high[...])
    )
    if early:
        for number, ref in enumerate(early):
            out[number * size:(number + 1) * size, :] = ref[...]
        out[first:first + size, :] = total
    else:
        out[...] = total


def shards(left_slots, right, previous, offsets, owners):
    own_block = left_slots[0]
    rows, width = own_block.shape
    count = offsets.shape[0]
    devices = lax.axis_size("row")
    columns = lax.axis_size("col")
    group = devices // 2
    size = rows // PARTS
    chunk = size // group

    def swap(array, mask):
        return lax.ppermute(array, "row", [(i, i ^ mask) for i in range(devices)])

    def shift(array, distance):
        pairs = [((i + distance) % columns, i) for i in range(columns)]
        return lax.ppermute(array, "col", pairs)

    shape = jax.ShapeDtypeStruct((count, chunk, width), own_block.dtype)

    def pick(pieces):
        return pl.pallas_call(
            functools.partial(pick_kernel, group),
            out_shape=(shape, shape),
            in_specs=[SMEM] + [VMEM] * len(pieces),
            out_specs=(VMEM, VMEM),
            compiler_params=PARAMS,
        )(owners, *pieces)

    def merge(low, high, mine, other):
        return pl.pallas_call(
            functools.partial(merge_kernel, low, high),
            out_shape=shape,
            in_specs=[SMEM, VMEM, VMEM],
            out_specs=VMEM,
            compiler_params=PARAMS,
        )(owners, mine, other)

    def multiply(part, pieces, rights, early):
        shape = (rows if early else size, right.shape[1])
        return pl.pallas_call(
            functools.partial(multiply_kernel, group, columns, part),
            out_shape=jax.ShapeDtypeStruct(shape, previous.dtype),
            in_specs=[SMEM, SMEM] + [VMEM] * (group + columns + 1 + len(early)),
            out_specs=VMEM,
            scratch_shapes=[
                pltpu.VMEM((size, count * width), jnp.bfloat16),
                pltpu.VMEM((size, count * width), jnp.bfloat16),
                pltpu.VMEM((count * width, right.shape[1]), jnp.bfloat16),
                pltpu.VMEM((count * width, right.shape[1]), jnp.bfloat16),
            ],
            compiler_params=PARAMS,
        )(offsets, owners, *pieces, *rights, previous, *early)

    picked = []
    for part in range(PARTS):
        start = part * size
        pieces = [own_block[start + s * chunk:start + (s + 2) * chunk] for s in range(0, group, 2)]
        for s in range(group // 2 - 1, 0, -1):
            pieces[s] = swap(pieces[s], 2 * s)
        keep, give = pick(pieces)
        picked.append(merge(1, 2, keep, swap(give, 1)))

    rights = [right] + [shift(right, distance) for distance in range(1, columns)]

    merged = [merge(group, devices, mine, swap(mine, group)) for mine in picked]

    results = []
    for part, mine in enumerate(merged):
        pieces = {0: mine}
        for s in range(group - 2, 0, -2):
            pieces[s] = swap(mine, s)
        for s in range(0, group, 2):
            pieces[s + 1] = swap(pieces[s], 1)
        early = results if part == PARTS - 1 else []
        results.append(multiply(part, [pieces[s] for s in range(group)], rights, early))
    return results[-1]


def solution(mesh):
    return jax.shard_map(
        shards,
        mesh=mesh,
        in_specs=(P("row", "col", None), P("col", "row"), P("col", "row"), P(), P("col", None)),
        out_specs=P("col", "row"),
        check_vma=False,
    )
```

```python
import functools

import jax
import jax.numpy as jnp
from jax import lax
from jax.experimental import pallas as pl
from jax.experimental.pallas import tpu as pltpu
from jax.sharding import PartitionSpec as P

PARTS = 2
VMEM = pl.BlockSpec(memory_space=pltpu.VMEM)
SMEM = pl.BlockSpec(memory_space=pltpu.SMEM)
ANY = pl.BlockSpec(memory_space=pl.ANY)


def call(kernel, out_shape, in_specs, operands, flops=0):
    outs = out_shape if isinstance(out_shape, tuple) else (out_shape,)
    moved = sum(x.size * x.dtype.itemsize for x in (*operands, *outs))
    return pl.pallas_call(
        kernel,
        out_shape=out_shape,
        in_specs=in_specs,
        out_specs=jax.tree.map(lambda _: VMEM, out_shape),
        cost_estimate=pl.CostEstimate(flops=flops, bytes_accessed=moved, transcendentals=0),
        compiler_params=pltpu.CompilerParams(vmem_limit_bytes=32 * 1024 * 1024),
    )(*operands)


def split(value):
    high = value.astype(jnp.bfloat16)
    low = (value - high.astype(jnp.float32)).astype(jnp.bfloat16)
    return high, low


def dot(left, right):
    return jnp.dot(left, right, preferred_element_type=jnp.float32)


def gather_kernel(part, chips, own, got, *refs):
    outs = refs[-(chips - 1):]
    chunk = outs[0].shape[1]
    for step, out in enumerate(outs, 1):
        place = part * chips + step
        out[0] = own[2 * place * chunk:(2 * place + 1) * chunk, :]
        out[1] = got[place * chunk:(place + 1) * chunk, :]


def pick_kernel(part, chips, owners, own, got, *refs):
    pieces, out = refs[:-1], refs[-1]
    chunk = out.shape[1]
    member = lax.axis_index("row") % (2 * chips)
    first = part * chips
    near = [own[2 * first * chunk:(2 * first + 1) * chunk, :], got[first * chunk:(first + 1) * chunk, :]]
    for number in range(out.shape[0]):
        mask = (owners[0, number] % (2 * chips)) ^ member
        for core in range(2):

            @pl.when(mask == core)
            def _():
                out[number] = near[core]

            for step, piece in enumerate(pieces, 1):

                @pl.when(mask == 2 * step + core)
                def _():
                    out[number] = piece[core]


def merge_kernel(group, owners, mine, other, out):
    half = lax.axis_index("row") // group
    for number in range(out.shape[0]):
        here = owners[0, number] // group == half

        @pl.when(here)
        def _():
            out[number] = mine[number]

        @pl.when(jnp.logical_not(here))
        def _():
            out[number] = other[number]


def right_kernel(offsets, *refs):
    rights, (right_high, right_low) = refs[:-2], refs[-2:]
    count = offsets.shape[0]
    width = right_high.shape[0] // count
    blocks = rights[0].shape[0] // width
    for number in range(count):
        lanes = slice(number * width, (number + 1) * width)
        for step, ref in enumerate(rights):
            for block in range(blocks):

                @pl.when(offsets[number] == step * blocks + block)
                def _():
                    high, low = split(ref[block * width:(block + 1) * width, :])
                    right_high[lanes, :] = high
                    right_low[lanes, :] = low


def multiply_kernel(part, owners, right_high, right_low, previous, *refs):
    group = len(refs) - part - 3
    pieces, early = refs[:group], refs[group:group + part]
    out, left_high, left_low = refs[group + part:]
    count, chunk, width = pieces[0].shape
    member = lax.axis_index("row") % group
    size = group * chunk
    for number in range(count):
        mask = (owners[0, number] % group) ^ member
        lanes = slice(number * width, (number + 1) * width)
        for step in range(group):
            place = pl.multiple_of((mask ^ step) * chunk, chunk)
            high, low = split(pieces[step][number])
            left_high[pl.ds(place, chunk), lanes] = high
            left_low[pl.ds(place, chunk), lanes] = low
    total = 2.0 * previous[part * size:(part + 1) * size, :] - (
        dot(left_high[...], right_low[...])
        + dot(left_low[...], right_high[...])
        + dot(left_high[...], right_high[...])
    )
    if out.shape[0] > size:
        for number, ref in enumerate(early):
            out[number * size:(number + 1) * size, :] = ref[...]
        out[part * size:, :] = total
    else:
        out[...] = total


def shards(left_slots, right, previous, offsets, owners):
    own = left_slots[0]
    rows, width = own.shape
    count = offsets.shape[0]
    devices = lax.axis_size("row")
    columns = lax.axis_size("col")
    group = devices // 2
    chips = group // 2
    size = rows // PARTS
    chunk = size // group
    piece = jax.ShapeDtypeStruct((count, chunk, width), own.dtype)
    pair = jax.ShapeDtypeStruct((2, chunk, width), own.dtype)

    def swap(array, mask):
        return lax.ppermute(array, "row", [(i, i ^ mask) for i in range(devices)])

    def shift(array, distance):
        pairs = [((i + distance) % columns, i) for i in range(columns)]
        return lax.ppermute(array, "col", pairs)

    got = swap(own.reshape(rows // (2 * chunk), 2 * chunk, width)[:, chunk:].reshape(rows // 2, width), 1)
    mine = []
    wait = []
    for part in range(PARTS):
        sent = call(
            functools.partial(gather_kernel, part, chips),
            (pair,) * (chips - 1),
            [VMEM, VMEM] + [ANY] * len(wait),
            (own, got, *wait),
        )
        pieces = [swap(array, 2 * step) for step, array in enumerate(sent, 1)]
        wait = pieces[-1:]
        mine.append(call(
            functools.partial(pick_kernel, part, chips),
            piece,
            [SMEM] + [VMEM] * (2 + len(pieces)),
            (owners, own, got, *pieces),
        ))

    rights = [right] + [shift(right, distance) for distance in range(1, columns)]
    terms = jax.ShapeDtypeStruct((count * width, right.shape[1]), jnp.bfloat16)
    right_terms = call(
        right_kernel, (terms, terms), [SMEM] + [VMEM] * columns, (offsets, *rights), flops=4 * terms.size
    )

    results = []
    for part in range(PARTS):
        merged = call(
            functools.partial(merge_kernel, group),
            piece,
            [SMEM, VMEM, VMEM],
            (owners, mine[part], swap(mine[part], group)),
        )
        pieces = {0: merged}
        step = chips
        while step > 1:
            for s in list(pieces):
                pieces[s + step] = swap(pieces[s], step)
            step //= 2
        for s in list(pieces):
            pieces[s + 1] = swap(pieces[s], 1)
        last = part == PARTS - 1
        operands = (owners, *right_terms, previous, *[pieces[s] for s in range(group)], *results)
        out_shape = jax.ShapeDtypeStruct((rows if last else size, right.shape[1]), previous.dtype)
        moved = sum(x.size * x.dtype.itemsize for x in operands)
        results.append(pl.pallas_call(
            functools.partial(multiply_kernel, part),
            out_shape=out_shape,
            in_specs=[SMEM] + [VMEM] * (len(operands) - 1),
            out_specs=VMEM,
            scratch_shapes=[pltpu.VMEM((size, count * width), jnp.bfloat16)] * 2,
            cost_estimate=pl.CostEstimate(
                flops=6 * size * count * width * right.shape[1], bytes_accessed=moved, transcendentals=0
            ),
            compiler_params=pltpu.CompilerParams(vmem_limit_bytes=32 * 1024 * 1024),
        )(*operands))
    return results[-1]


def solution(mesh):
    return jax.shard_map(
        shards,
        mesh=mesh,
        in_specs=(P("row", "col", None), P("col", "row"), P("col", "row"), P(), P("col", None)),
        out_specs=P("col", "row"),
        check_vma=False,
    )
```

```python
import functools

import jax
import jax.numpy as jnp
from jax import lax
from jax.experimental import pallas as pl
from jax.experimental.pallas import tpu as pltpu
from jax.sharding import PartitionSpec as P

PARTS = 2
VMEM = pl.BlockSpec(memory_space=pltpu.VMEM)
SMEM = pl.BlockSpec(memory_space=pltpu.SMEM)
ANY = pl.BlockSpec(memory_space=pl.ANY)


def call(kernel, out_shape, in_specs, operands, flops=0):
    outs = out_shape if isinstance(out_shape, tuple) else (out_shape,)
    moved = sum(x.size * x.dtype.itemsize for x in (*operands, *outs))
    return pl.pallas_call(
        kernel,
        out_shape=out_shape,
        in_specs=in_specs,
        out_specs=jax.tree.map(lambda _: VMEM, out_shape),
        cost_estimate=pl.CostEstimate(flops=flops, bytes_accessed=moved, transcendentals=0),
        compiler_params=pltpu.CompilerParams(vmem_limit_bytes=32 * 1024 * 1024),
    )(*operands)


def split(value):
    high = value.astype(jnp.bfloat16)
    low = (value - high.astype(jnp.float32)).astype(jnp.bfloat16)
    return high, low


def dot(left, right):
    return jnp.dot(left, right, preferred_element_type=jnp.float32)


def gather_kernel(part, chips, own, got, *refs):
    outs = refs[-(chips - 1):]
    chunk = outs[0].shape[1]
    for step, out in enumerate(outs, 1):
        place = part * chips + step
        out[0] = own[2 * place * chunk:(2 * place + 1) * chunk, :]
        out[1] = got[place * chunk:(place + 1) * chunk, :]


def pick(part, chips, owners, own, got, pieces, out):
    chunk = out.shape[1]
    member = lax.axis_index("row") % (2 * chips)
    first = part * chips
    near = [own[2 * first * chunk:(2 * first + 1) * chunk, :], got[first * chunk:(first + 1) * chunk, :]]
    for number in range(out.shape[0]):
        mask = (owners[0, number] % (2 * chips)) ^ member
        for core in range(2):

            @pl.when(mask == core)
            def _():
                out[number] = near[core]

            for step, piece in enumerate(pieces, 1):

                @pl.when(mask == 2 * step + core)
                def _():
                    out[number] = piece[core]


def merge(group, owners, mine, other, out):
    half = lax.axis_index("row") // group
    for number in range(out.shape[0]):
        here = owners[0, number] // group == half

        @pl.when(here)
        def _():
            out[number] = mine[number]

        @pl.when(jnp.logical_not(here))
        def _():
            out[number] = other[number]


def pick_kernel(chips, owners, own, got, *refs):
    pick(0, chips, owners, own, got, refs[:chips - 1], refs[-1])


def step_kernel(part, chips, owners, mine, other, own, got, *refs):
    pick(part, chips, owners, own, got, refs[:chips - 1], refs[-1])
    merge(2 * chips, owners, mine, other, refs[-2])


def merge_kernel(group, owners, mine, other, *refs):
    merge(group, owners, mine, other, refs[-1])


def right_kernel(offsets, *refs):
    rights, (right_high, right_low) = refs[:-2], refs[-2:]
    count = offsets.shape[0]
    width = right_high.shape[0] // count
    blocks = rights[0].shape[0] // width
    for number in range(count):
        lanes = slice(number * width, (number + 1) * width)
        for step, ref in enumerate(rights):
            for block in range(blocks):

                @pl.when(offsets[number] == step * blocks + block)
                def _():
                    high, low = split(ref[block * width:(block + 1) * width, :])
                    right_high[lanes, :] = high
                    right_low[lanes, :] = low


def multiply_kernel(part, owners, right_high, right_low, previous, *refs):
    group = len(refs) - part - 3
    pieces, early = refs[:group], refs[group:group + part]
    out, left_high, left_low = refs[group + part:]
    count, chunk, width = pieces[0].shape
    member = lax.axis_index("row") % group
    size = group * chunk
    for number in range(count):
        mask = (owners[0, number] % group) ^ member
        lanes = slice(number * width, (number + 1) * width)
        for step in range(group):
            place = pl.multiple_of((mask ^ step) * chunk, chunk)
            high, low = split(pieces[step][number])
            left_high[pl.ds(place, chunk), lanes] = high
            left_low[pl.ds(place, chunk), lanes] = low
    total = 2.0 * previous[part * size:(part + 1) * size, :] - (
        dot(left_high[...], right_low[...])
        + dot(left_low[...], right_high[...])
        + dot(left_high[...], right_high[...])
    )
    if out.shape[0] > size:
        for number, ref in enumerate(early):
            out[number * size:(number + 1) * size, :] = ref[...]
        out[part * size:, :] = total
    else:
        out[...] = total


def shards(left_slots, right, previous, offsets, owners):
    own = left_slots[0]
    rows, width = own.shape
    count = offsets.shape[0]
    devices = lax.axis_size("row")
    columns = lax.axis_size("col")
    group = devices // 2
    chips = group // 2
    size = rows // PARTS
    chunk = size // group
    piece = jax.ShapeDtypeStruct((count, chunk, width), own.dtype)
    pair = jax.ShapeDtypeStruct((2, chunk, width), own.dtype)

    def swap(array, mask):
        return lax.ppermute(array, "row", [(i, i ^ mask) for i in range(devices)])

    def shift(array, distance):
        pairs = [((i + distance) % columns, i) for i in range(columns)]
        return lax.ppermute(array, "col", pairs)

    got = swap(own.reshape(rows // (2 * chunk), 2 * chunk, width)[:, chunk:].reshape(rows // 2, width), 1)
    arrived = []
    for part in range(PARTS):
        wait = [arrived[-1][-1]] if arrived else []
        sent = call(
            functools.partial(gather_kernel, part, chips),
            (pair,) * (chips - 1),
            [VMEM, VMEM] + [ANY] * len(wait),
            (own, got, *wait),
        )
        arrived.append([swap(array, 2 * step) for step, array in enumerate(sent, 1)])

    rights = [right] + [shift(right, distance) for distance in range(1, columns)]
    terms = jax.ShapeDtypeStruct((count * width, right.shape[1]), jnp.bfloat16)
    right_terms = call(
        right_kernel, (terms, terms), [SMEM] + [VMEM] * columns, (offsets, *rights), flops=4 * terms.size
    )

    mine = call(
        functools.partial(pick_kernel, chips), piece, [SMEM] + [VMEM] * (chips + 1), (owners, own, got, *arrived[0])
    )
    def spread(merged):
        pieces = {0: merged}
        step = chips
        while step > 1:
            for s in list(pieces):
                pieces[s + step] = swap(pieces[s], step)
            step //= 2
        return pieces

    gathered = []
    for part in range(1, PARTS):
        merged, mine = call(
            functools.partial(step_kernel, part, chips),
            (piece, piece),
            [SMEM] + [VMEM] * (chips + 3),
            (owners, mine, swap(mine, group), own, got, *arrived[part]),
        )
        gathered.append(spread(merged))
    wait = [right_terms[0]] + [array for pieces in gathered for s, array in pieces.items() if s]
    merged = call(
        functools.partial(merge_kernel, group),
        piece,
        [SMEM, VMEM, VMEM] + [ANY] * len(wait),
        (owners, mine, swap(mine, group), *wait),
    )
    gathered.append(spread(merged))

    results = []
    for part, pieces in enumerate(gathered):
        for s in list(pieces):
            pieces[s + 1] = swap(pieces[s], 1)
        last = part == PARTS - 1
        operands = (owners, *right_terms, previous, *[pieces[s] for s in range(group)], *results)
        out_shape = jax.ShapeDtypeStruct((rows if last else size, right.shape[1]), previous.dtype)
        moved = sum(x.size * x.dtype.itemsize for x in operands)
        results.append(pl.pallas_call(
            functools.partial(multiply_kernel, part),
            out_shape=out_shape,
            in_specs=[SMEM] + [VMEM] * (len(operands) - 1),
            out_specs=VMEM,
            scratch_shapes=[pltpu.VMEM((size, count * width), jnp.bfloat16)] * 2,
            cost_estimate=pl.CostEstimate(
                flops=6 * size * count * width * right.shape[1], bytes_accessed=moved, transcendentals=0
            ),
            compiler_params=pltpu.CompilerParams(vmem_limit_bytes=32 * 1024 * 1024),
        )(*operands))
    return results[-1]


def solution(mesh):
    return jax.shard_map(
        shards,
        mesh=mesh,
        in_specs=(P("row", "col", None), P("col", "row"), P("col", "row"), P(), P("col", None)),
        out_specs=P("col", "row"),
        check_vma=False,
    )
```

```python
import functools

import jax
import jax.numpy as jnp
from jax import lax
from jax.experimental import pallas as pl
from jax.experimental.pallas import tpu as pltpu
from jax.sharding import PartitionSpec as P

VMEM = pl.BlockSpec(memory_space=pltpu.VMEM)
SMEM = pl.BlockSpec(memory_space=pltpu.SMEM)
ANY = pl.BlockSpec(memory_space=pl.ANY)


def call(kernel, out_shape, in_specs, operands, flops=0, scratch=()):
    outs = out_shape if isinstance(out_shape, tuple) else (out_shape,)
    moved = sum(x.size * x.dtype.itemsize for x in (*operands, *outs))
    return pl.pallas_call(
        kernel,
        out_shape=out_shape,
        in_specs=in_specs,
        out_specs=jax.tree.map(lambda _: VMEM, out_shape),
        scratch_shapes=scratch,
        cost_estimate=pl.CostEstimate(flops=flops, bytes_accessed=moved, transcendentals=0),
        compiler_params=pltpu.CompilerParams(vmem_limit_bytes=32 * 1024 * 1024),
    )(*operands)


def split(value):
    high = value.astype(jnp.bfloat16)
    low = (value - high.astype(jnp.float32)).astype(jnp.bfloat16)
    return high, low


def dot(left, right):
    return jnp.dot(left, right, preferred_element_type=jnp.float32)


def flag_kernel(group, few, owners, out):
    count = owners.shape[1]
    same = jnp.int32(0)
    upper = jnp.int32(0)
    for number in range(count):
        upper += owners[0, number] // group
        for other in range(number):
            same = jnp.where(owners[0, number] // 2 == owners[0, other] // 2, 1, same)
    many = jnp.where(jnp.maximum(upper, count - upper) > few, 2, 0)
    out[...] = jnp.full(out.shape, same + many, jnp.int32)


def gather_kernel(chips, own, got, *outs):
    chunk = outs[0].shape[1]
    for step, out in enumerate(outs, 1):
        out[0] = own[2 * step * chunk:(2 * step + 1) * chunk, :]
        out[1] = got[step * chunk:(step + 1) * chunk, :]


def gather_one_kernel(chips, owners, own, got, *outs):
    chunk = outs[0].shape[0]
    index = lax.axis_index("row")
    mine = jnp.int32(0)
    for number in range(owners.shape[1]):
        mine = jnp.where(owners[0, number] == index, 1, mine)

    @pl.when(mine == 1)
    def _():
        for step, out in enumerate(outs, 1):
            out[...] = own[2 * step * chunk:(2 * step + 1) * chunk, :]

    @pl.when(mine == 0)
    def _():
        for step, out in enumerate(outs, 1):
            out[...] = got[step * chunk:(step + 1) * chunk, :]


def pick_kernel(chips, owners, own, got, *refs):
    pieces, out = refs[:-1], refs[-1]
    chunk = out.shape[1]
    member = lax.axis_index("row") % (2 * chips)
    near = [own[:chunk, :], got[:chunk, :]]
    for number in range(out.shape[0]):
        mask = (owners[0, number] % (2 * chips)) ^ member
        for core in range(2):

            @pl.when(mask == core)
            def _():
                out[number] = near[core]

        for step, piece in enumerate(pieces, 1):
            if len(piece.shape) == 2:

                @pl.when(mask // 2 == step)
                def _():
                    out[number] = piece[...]
            else:
                for core in range(2):

                    @pl.when(mask == 2 * step + core)
                    def _():
                        out[number] = piece[core]


def pack_kernel(group, owners, mine, out):
    half = lax.axis_index("row") // group
    before = jnp.int32(0)
    for number in range(mine.shape[0]):
        here = owners[0, number] // group == half
        for slot in range(min(number + 1, out.shape[0])):

            @pl.when(here & (before == slot))
            def _():
                out[slot] = mine[number]

        before = jnp.where(here, before + 1, before)


def merge_kernel(group, owners, mine, other, out):
    half = lax.axis_index("row") // group
    packed = other.shape[0] < out.shape[0]
    before = jnp.int32(0)
    for number in range(out.shape[0]):
        here = owners[0, number] // group == half

        @pl.when(here)
        def _():
            out[number] = mine[number]

        if packed:
            for slot in range(min(number + 1, other.shape[0])):

                @pl.when(jnp.logical_not(here) & (before == slot))
                def _():
                    out[number] = other[slot]

            before = jnp.where(here, before, before + 1)
        else:

            @pl.when(jnp.logical_not(here))
            def _():
                out[number] = other[number]


def right_kernel(offsets, *refs):
    rights, (right_high, right_low) = refs[:-2], refs[-2:]
    count = offsets.shape[0]
    width = right_high.shape[0] // count
    blocks = rights[0].shape[0] // width
    for number in range(count):
        lanes = slice(number * width, (number + 1) * width)
        for step, ref in enumerate(rights):
            for block in range(blocks):

                @pl.when(offsets[number] == step * blocks + block)
                def _():
                    high, low = split(ref[block * width:(block + 1) * width, :])
                    right_high[lanes, :] = high
                    right_low[lanes, :] = low


def multiply_kernel(group, steps, owners, right_high, right_low, previous, *refs):
    pieces, (out, left_high, left_low) = refs[:-3], refs[-3:]
    count, chunk, width = pieces[0].shape
    member = lax.axis_index("row") % group
    for number in range(count):
        mask = (owners[0, number] % group) ^ member
        lanes = slice(number * width, (number + 1) * width)
        for (step, shift), piece in zip(steps, pieces):
            size = piece.shape[1]
            place = pl.multiple_of((mask ^ step) * chunk + shift, size)
            high, low = split(piece[number])
            left_high[pl.ds(place, size), lanes] = high
            left_low[pl.ds(place, size), lanes] = low
    out[...] = 2.0 * previous[...] - (
        dot(left_high[...], right_low[...])
        + dot(left_low[...], right_high[...])
        + dot(left_high[...], right_high[...])
    )


def shards(left_slots, right, previous, offsets, owners):
    own = left_slots[0]
    rows, width = own.shape
    count = offsets.shape[0]
    devices = lax.axis_size("row")
    columns = lax.axis_size("col")
    group = devices // 2
    chips = group // 2
    chunk = rows // group
    few = (2 * count + 2) // 3
    bits = [1 << b for b in range(1, group.bit_length() - 1)]

    def shape(*dims):
        return jax.ShapeDtypeStruct(dims, own.dtype)

    def swap(array, mask):
        return lax.ppermute(array, "row", [(i, i ^ mask) for i in range(devices)])

    def shift(array, distance):
        pairs = [((i + distance) % columns, i) for i in range(columns)]
        return lax.ppermute(array, "col", pairs)

    got = swap(own.reshape(chips, 2 * chunk, width)[:, chunk:].reshape(rows // 2, width), 1)

    flags = call(
        functools.partial(flag_kernel, group, few), jax.ShapeDtypeStruct((8, 128), jnp.int32), [SMEM], (owners,)
    )
    distance = 1
    while distance < columns:
        flags = flags | shift(flags, distance)
        distance *= 2
    flag = flags[0, 0]

    def pick(sent):
        pieces = [swap(array, 2 * step) for step, array in enumerate(sent, 1)]
        return call(
            functools.partial(pick_kernel, chips),
            shape(count, chunk, width),
            [SMEM] + [VMEM] * (chips + 1),
            (owners, own, got, *pieces),
        )

    def pick_two():
        kernel = functools.partial(gather_kernel, chips)
        return pick(call(kernel, (shape(2, chunk, width),) * (chips - 1), [VMEM, VMEM], (own, got)))

    def pick_one():
        kernel = functools.partial(gather_one_kernel, chips)
        return pick(call(kernel, (shape(chunk, width),) * (chips - 1), [SMEM, VMEM, VMEM], (owners, own, got)))

    mine = lax.cond(flag & 1 == 1, pick_two, pick_one)

    def merge(mine, sent):
        return call(
            functools.partial(merge_kernel, group),
            shape(count, chunk, width),
            [SMEM, VMEM, VMEM],
            (owners, mine, swap(sent, group)),
        )

    def merge_all(mine):
        return merge(mine, mine)

    def merge_few(mine):
        kernel = functools.partial(pack_kernel, group)
        return merge(mine, call(kernel, shape(few, chunk, width), [SMEM, VMEM], (owners, mine)))

    merged = lax.cond(flag & 2 == 2, merge_all, merge_few, mine)

    rights = [right] + [shift(right, distance) for distance in range(1, columns)]
    terms = jax.ShapeDtypeStruct((count * width, right.shape[1]), jnp.bfloat16)
    right_terms = call(
        right_kernel, (terms, terms), [SMEM] + [VMEM] * columns, (offsets, *rights), flops=4 * terms.size
    )

    cut = chunk // 2
    pieces = {0: [merged]}
    for s in sorted(range(2, group, 2), key=lambda s: (s.bit_count(), -s)):
        if s.bit_count() == 1:
            pieces[s] = [swap(merged, s)]
        else:
            low, high = s & -s, 1 << (s.bit_length() - 1)
            first, second = pieces[s ^ low], pieces[s ^ high]
            first = first[0] if len(first) == 2 else first[0][:, :cut]
            second = second[1] if len(second) == 2 else second[0][:, cut:]
            pieces[s] = [swap(first, low), swap(second, high)]
    for s in list(pieces):
        pieces[s + 1] = [swap(array, 1) for array in pieces[s]]

    steps = [(s, i * cut) for s in pieces for i in range(len(pieces[s]))]
    flat = [array for s in pieces for array in pieces[s]]
    return call(
        functools.partial(multiply_kernel, group, steps),
        jax.ShapeDtypeStruct(previous.shape, previous.dtype),
        [SMEM] + [VMEM] * (3 + len(flat)),
        (owners, *right_terms, previous, *flat),
        flops=6 * rows * count * width * right.shape[1],
        scratch=[pltpu.VMEM((rows, count * width), jnp.bfloat16)] * 2,
    )


def solution(mesh):
    return jax.shard_map(
        shards,
        mesh=mesh,
        in_specs=(P("row", "col", None), P("col", "row"), P("col", "row"), P(), P("col", None)),
        out_specs=P("col", "row"),
        check_vma=False,
    )
```

```python
import functools

import jax
import jax.numpy as jnp
from jax import lax
from jax.experimental import pallas as pl
from jax.experimental.pallas import tpu as pltpu
from jax.sharding import PartitionSpec as P

PARTS = 2
VMEM = pl.BlockSpec(memory_space=pltpu.VMEM)
SMEM = pl.BlockSpec(memory_space=pltpu.SMEM)
ANY = pl.BlockSpec(memory_space=pl.ANY)


def call(kernel, out_shape, in_specs, operands, flops=0, scratch=()):
    outs = out_shape if isinstance(out_shape, tuple) else (out_shape,)
    moved = sum(x.size * x.dtype.itemsize for x in (*operands, *outs))
    return pl.pallas_call(
        kernel,
        out_shape=out_shape,
        in_specs=in_specs,
        out_specs=jax.tree.map(lambda _: VMEM, out_shape),
        scratch_shapes=scratch,
        cost_estimate=pl.CostEstimate(flops=flops, bytes_accessed=moved, transcendentals=0),
        compiler_params=pltpu.CompilerParams(vmem_limit_bytes=32 * 1024 * 1024),
    )(*operands)


def split(value):
    high = value.astype(jnp.bfloat16)
    low = (value - high.astype(jnp.float32)).astype(jnp.bfloat16)
    return high, low


def dot(left, right):
    return jnp.dot(left, right, preferred_element_type=jnp.float32)


def flag_kernel(group, few, owners, out):
    count = owners.shape[1]
    upper = jnp.int32(0)
    for number in range(count):
        upper += owners[0, number] // group
    many = jnp.where(jnp.maximum(upper, count - upper) > few, 1, 0)
    out[...] = jnp.full(out.shape, many, jnp.int32)


def copy_kernel(array, *refs):
    refs[-1][...] = array[...]


def gather_kernel(chips, own, got, *outs):
    parts, _, chunk, _ = outs[0].shape
    for step, out in enumerate(outs, 1):
        for part in range(parts):
            place = part * chips + step
            out[part, 0] = own[2 * place * chunk:(2 * place + 1) * chunk, :]
            out[part, 1] = got[place * chunk:(place + 1) * chunk, :]


def pick(part, chips, owners, own, got, pieces, outs):
    out, packed = outs[0], outs[1:]
    chunk = out.shape[1]
    group = 2 * chips
    index = lax.axis_index("row")
    first = part * chips * chunk
    before = jnp.int32(0)
    for number in range(out.shape[0]):
        owner = owners[0, number]
        mask = (owner % group) ^ (index % group)
        here = owner // group == index // group

        def put(read):
            out[number] = read()
            for ref in packed:
                for slot in range(min(number + 1, ref.shape[0])):

                    @pl.when(here & (before == slot))
                    def _():
                        ref[slot] = read()

        @pl.when(mask == 0)
        def _():
            put(lambda: own[2 * first:2 * first + chunk, :])

        @pl.when(mask == 1)
        def _():
            put(lambda: got[first:first + chunk, :])

        for step, piece in enumerate(pieces, 1):
            for core in range(2):

                @pl.when(mask == 2 * step + core)
                def _():
                    put(lambda: piece[part, core])

        before = jnp.where(here, before + 1, before)


def merge(group, owners, mine, other, out):
    half = lax.axis_index("row") // group
    packed = other.shape[0] < out.shape[0]
    before = jnp.int32(0)
    for number in range(out.shape[0]):
        here = owners[0, number] // group == half

        @pl.when(here)
        def _():
            out[number] = mine[number]

        if packed:
            for slot in range(min(number + 1, other.shape[0])):

                @pl.when(jnp.logical_not(here) & (before == slot))
                def _():
                    out[number] = other[slot]

            before = jnp.where(here, before, before + 1)
        else:

            @pl.when(jnp.logical_not(here))
            def _():
                out[number] = other[number]


def pick_kernel(chips, owners, own, got, *refs):
    pick(0, chips, owners, own, got, refs[:chips - 1], refs[chips - 1:])


def step_kernel(part, chips, owners, mine, other, own, got, *refs):
    pick(part, chips, owners, own, got, refs[:chips - 1], refs[chips:])
    merge(2 * chips, owners, mine, other, refs[chips - 1])


def merge_kernel(group, owners, mine, other, *refs):
    merge(group, owners, mine, other, refs[-1])


def right_kernel(offsets, *refs):
    sources, (right_high, right_low) = refs[:-2], refs[-2:]
    count = offsets.shape[0]
    width = right_high.shape[0] // count
    blocks = [ref.at[place:place + width] for ref in sources for place in range(0, ref.shape[0], width)]
    for number in range(count):
        lanes = slice(number * width, (number + 1) * width)
        for block, ref in enumerate(blocks):

            @pl.when(offsets[number] == block)
            def _():
                high, low = split(ref[...])
                right_high[lanes, :] = high
                right_low[lanes, :] = low


def multiply_kernel(part, group, owners, right_high, right_low, previous, *refs):
    pieces, early = refs[:group], refs[group:-3]
    out, left_high, left_low = refs[-3:]
    count, chunk, width = pieces[0].shape
    member = lax.axis_index("row") % group
    size = group * chunk
    for number in range(count):
        mask = (owners[0, number] % group) ^ member
        lanes = slice(number * width, (number + 1) * width)
        for step in range(group):
            place = pl.multiple_of((mask ^ step) * chunk, chunk)
            high, low = split(pieces[step][number])
            left_high[pl.ds(place, chunk), lanes] = high
            left_low[pl.ds(place, chunk), lanes] = low
    total = 2.0 * previous[part * size:(part + 1) * size, :] - (
        dot(left_high[...], right_low[...])
        + dot(left_low[...], right_high[...])
        + dot(left_high[...], right_high[...])
    )
    if out.shape[0] > size:
        for number, ref in enumerate(early):
            out[number * size:(number + 1) * size, :] = ref[...]
        out[part * size:, :] = total
    else:
        out[...] = total


def shards(left_slots, right, previous, offsets, owners):
    own = left_slots[0]
    rows, width = own.shape
    count = offsets.shape[0]
    devices = lax.axis_size("row")
    columns = lax.axis_size("col")
    group = devices // 2
    chips = group // 2
    size = rows // PARTS
    chunk = size // group
    few = (2 * count + 2) // 3

    def shape(*dims):
        return jax.ShapeDtypeStruct(dims, own.dtype)

    def swap(array, mask):
        return lax.ppermute(array, "row", [(i, i ^ mask) for i in range(devices)])

    def shift(array, distance):
        pairs = [((i + distance) % columns, i) for i in range(columns)]
        return lax.ppermute(array, "col", pairs)

    def copy(array, wait):
        return call(copy_kernel, jax.ShapeDtypeStruct(array.shape, array.dtype), [VMEM, ANY], (array, wait))

    got = swap(own.reshape(PARTS * chips, 2 * chunk, width)[:, chunk:].reshape(rows // 2, width), 1)
    sent = call(
        functools.partial(gather_kernel, chips),
        (shape(PARTS, 2, chunk, width),) * (chips - 1),
        [VMEM, VMEM],
        (own, got),
    )
    arrived = [swap(array, 2 * step) for step, array in enumerate(sent, 1)]

    flags = call(
        functools.partial(flag_kernel, group, few), jax.ShapeDtypeStruct((8, 128), jnp.int32), [SMEM], (owners,)
    )
    distance = 1
    while distance < columns:
        flags = flags | shift(flags, distance)
        distance *= 2

    rest = right.shape[0] - width
    last = right[rest:]
    last_blocks = [shift(last, distance) for distance in range(1, columns)]

    def finish(slots):
        packed = (shape(slots, chunk, width),) if slots < count else ()
        piece = shape(count, chunk, width)
        picked = call(
            functools.partial(pick_kernel, chips),
            (piece, *packed),
            [SMEM] + [VMEM] * (chips + 1),
            (owners, own, got, *arrived),
        )

        sources = [right]
        if rest:
            first_blocks = copy(right[:rest], picked[0])
        for distance, block in enumerate(last_blocks, 1):
            sources += [shift(first_blocks, distance), block] if rest else [block]
        terms = jax.ShapeDtypeStruct((count * width, right.shape[1]), jnp.bfloat16)
        right_terms = call(
            right_kernel, (terms, terms), [SMEM] + [VMEM] * len(sources), (offsets, *sources), flops=4 * terms.size
        )

        def spread(part, merged):
            pieces = {0: merged}
            bits = [1 << b for b in range(1, group.bit_length() - 1)]
            for bit in bits if part % 2 else reversed(bits):
                for s in list(pieces):
                    pieces[s + bit] = swap(pieces[s], bit)
            return pieces

        gathered = []
        for part in range(1, PARTS):
            merged, *following = call(
                functools.partial(step_kernel, part, chips),
                (piece, piece, *packed),
                [SMEM] + [VMEM] * (chips + 3),
                (owners, picked[0], swap(picked[-1], group), own, got, *arrived),
            )
            picked = following
            gathered.append(spread(part - 1, merged))
        wait = [array for pieces in gathered for s, array in pieces.items() if s]
        merged = call(
            functools.partial(merge_kernel, group),
            piece,
            [SMEM, VMEM, VMEM] + [ANY] * len(wait),
            (owners, picked[0], swap(picked[-1], group), *wait),
        )
        gathered.append(spread(PARTS - 1, merged))

        results = []
        for part, pieces in enumerate(gathered):
            for s in list(pieces):
                pieces[s + 1] = swap(pieces[s], 1)
            early = results if part == PARTS - 1 else []
            operands = (owners, *right_terms, previous, *[pieces[s] for s in range(group)], *early)
            results.append(call(
                functools.partial(multiply_kernel, part, group),
                jax.ShapeDtypeStruct((rows if early else size, right.shape[1]), previous.dtype),
                [SMEM] + [VMEM] * (len(operands) - 1),
                operands,
                flops=6 * size * count * width * right.shape[1],
                scratch=[pltpu.VMEM((size, count * width), jnp.bfloat16)] * 2,
            ))
        return results[-1]

    return lax.cond(flags[0, 0] == 0, lambda: finish(few), lambda: finish(count))


def solution(mesh):
    return jax.shard_map(
        shards,
        mesh=mesh,
        in_specs=(P("row", "col", None), P("col", "row"), P("col", "row"), P(), P("col", None)),
        out_specs=P("col", "row"),
        check_vma=False,
    )
```

```python
import functools

import jax
import jax.numpy as jnp
from jax import lax
from jax.experimental import pallas as pl
from jax.experimental.pallas import tpu as pltpu
from jax.sharding import PartitionSpec as P

PARTS = 2
VMEM = pl.BlockSpec(memory_space=pltpu.VMEM)
SMEM = pl.BlockSpec(memory_space=pltpu.SMEM)
ANY = pl.BlockSpec(memory_space=pl.ANY)


def call(kernel, out_shape, in_specs, operands, flops=0):
    outs = out_shape if isinstance(out_shape, tuple) else (out_shape,)
    moved = sum(x.size * x.dtype.itemsize for x in (*operands, *outs))
    return pl.pallas_call(
        kernel,
        out_shape=out_shape,
        in_specs=in_specs,
        out_specs=jax.tree.map(lambda _: VMEM, out_shape),
        cost_estimate=pl.CostEstimate(flops=flops, bytes_accessed=moved, transcendentals=0),
        compiler_params=pltpu.CompilerParams(vmem_limit_bytes=32 * 1024 * 1024),
    )(*operands)


def split(value):
    high = value.astype(jnp.bfloat16)
    low = (value - high.astype(jnp.float32)).astype(jnp.bfloat16)
    return high, low


def dot(left, right):
    return jnp.dot(left, right, preferred_element_type=jnp.float32)


def gather_kernel(part, chips, own, got, *refs):
    outs = refs[-(chips - 1):]
    chunk = outs[0].shape[1]
    for step, out in enumerate(outs, 1):
        place = part * chips + step
        out[0] = own[2 * place * chunk:(2 * place + 1) * chunk, :]
        out[1] = got[place * chunk:(place + 1) * chunk, :]


def pick_kernel(part, chips, owners, own, got, *refs):
    pieces, out = refs[:-1], refs[-1]
    chunk = out.shape[1]
    member = lax.axis_index("row") % (2 * chips)
    first = part * chips
    near = [own[2 * first * chunk:(2 * first + 1) * chunk, :], got[first * chunk:(first + 1) * chunk, :]]
    for number in range(out.shape[0]):
        mask = (owners[0, number] % (2 * chips)) ^ member
        for core in range(2):

            @pl.when(mask == core)
            def _():
                out[number] = near[core]

            for step, piece in enumerate(pieces, 1):

                @pl.when(mask == 2 * step + core)
                def _():
                    out[number] = piece[core]


def merge_kernel(group, owners, mine, other, *refs):
    out = refs[-1]
    half = lax.axis_index("row") // group
    for number in range(out.shape[0]):
        here = owners[0, number] // group == half

        @pl.when(here)
        def _():
            out[number] = mine[number]

        @pl.when(jnp.logical_not(here))
        def _():
            out[number] = other[number]


def right_kernel(offsets, *refs):
    rights, (right_high, right_low) = refs[:-2], refs[-2:]
    count = offsets.shape[0]
    width = right_high.shape[0] // count
    blocks = rights[0].shape[0] // width
    for number in range(count):
        lanes = slice(number * width, (number + 1) * width)
        for step, ref in enumerate(rights):
            for block in range(blocks):

                @pl.when(offsets[number] == step * blocks + block)
                def _():
                    high, low = split(ref[block * width:(block + 1) * width, :])
                    right_high[lanes, :] = high
                    right_low[lanes, :] = low


def multiply_kernel(part, owners, right_high, right_low, previous, *refs):
    group = len(refs) - part - 3
    pieces, early = refs[:group], refs[group:group + part]
    out, left_high, left_low = refs[group + part:]
    count, chunk, width = pieces[0].shape
    member = lax.axis_index("row") % group
    size = group * chunk
    for number in range(count):
        mask = (owners[0, number] % group) ^ member
        lanes = slice(number * width, (number + 1) * width)
        for step in range(group):
            place = pl.multiple_of((mask ^ step) * chunk, chunk)
            high, low = split(pieces[step][number])
            left_high[pl.ds(place, chunk), lanes] = high
            left_low[pl.ds(place, chunk), lanes] = low
    total = 2.0 * previous[part * size:(part + 1) * size, :] - (
        dot(left_high[...], right_low[...])
        + dot(left_low[...], right_high[...])
        + dot(left_high[...], right_high[...])
    )
    if out.shape[0] > size:
        for number, ref in enumerate(early):
            out[number * size:(number + 1) * size, :] = ref[...]
        out[part * size:, :] = total
    else:
        out[...] = total


def shards(left_slots, right, previous, offsets, owners):
    own = left_slots[0]
    rows, width = own.shape
    count = offsets.shape[0]
    devices = lax.axis_size("row")
    columns = lax.axis_size("col")
    group = devices // 2
    chips = group // 2
    size = rows // PARTS
    chunk = size // group
    piece = jax.ShapeDtypeStruct((count, chunk, width), own.dtype)
    pair = jax.ShapeDtypeStruct((2, chunk, width), own.dtype)

    def swap(array, mask):
        return lax.ppermute(array, "row", [(i, i ^ mask) for i in range(devices)])

    def shift(array, distance):
        pairs = [((i + distance) % columns, i) for i in range(columns)]
        return lax.ppermute(array, "col", pairs)

    got = swap(own.reshape(rows // (2 * chunk), 2 * chunk, width)[:, chunk:].reshape(rows // 2, width), 1)
    mine = []
    wait = []
    for part in range(PARTS):
        sent = call(
            functools.partial(gather_kernel, part, chips),
            (pair,) * (chips - 1),
            [VMEM, VMEM] + [ANY] * len(wait),
            (own, got, *wait),
        )
        pieces = [swap(array, 2 * step) for step, array in enumerate(sent, 1)]
        wait = pieces[-1:]
        mine.append(call(
            functools.partial(pick_kernel, part, chips),
            piece,
            [SMEM] + [VMEM] * (2 + len(pieces)),
            (owners, own, got, *pieces),
        ))

    rights = [right] + [shift(right, distance) for distance in range(1, columns)]
    terms = jax.ShapeDtypeStruct((count * width, right.shape[1]), jnp.bfloat16)
    right_terms = call(
        right_kernel, (terms, terms), [SMEM] + [VMEM] * columns, (offsets, *rights), flops=4 * terms.size
    )

    results = []
    for part in range(PARTS):
        wait = right_terms[:1] if part == PARTS - 1 else ()
        merged = call(
            functools.partial(merge_kernel, group),
            piece,
            [SMEM, VMEM, VMEM] + [ANY] * len(wait),
            (owners, mine[part], swap(mine[part], group), *wait),
        )
        pieces = {0: merged}
        bits = [1 << b for b in range(1, group.bit_length() - 1)]
        for bit in bits if part % 2 else reversed(bits):
            for s in list(pieces):
                pieces[s + bit] = swap(pieces[s], bit)
        for s in list(pieces):
            pieces[s + 1] = swap(pieces[s], 1)
        last = part == PARTS - 1
        operands = (owners, *right_terms, previous, *[pieces[s] for s in range(group)], *results)
        out_shape = jax.ShapeDtypeStruct((rows if last else size, right.shape[1]), previous.dtype)
        moved = sum(x.size * x.dtype.itemsize for x in operands)
        results.append(pl.pallas_call(
            functools.partial(multiply_kernel, part),
            out_shape=out_shape,
            in_specs=[SMEM] + [VMEM] * (len(operands) - 1),
            out_specs=VMEM,
            scratch_shapes=[pltpu.VMEM((size, count * width), jnp.bfloat16)] * 2,
            cost_estimate=pl.CostEstimate(
                flops=6 * size * count * width * right.shape[1], bytes_accessed=moved, transcendentals=0
            ),
            compiler_params=pltpu.CompilerParams(vmem_limit_bytes=32 * 1024 * 1024),
        )(*operands))
    return results[-1]


def solution(mesh):
    return jax.shard_map(
        shards,
        mesh=mesh,
        in_specs=(P("row", "col", None), P("col", "row"), P("col", "row"), P(), P("col", None)),
        out_specs=P("col", "row"),
        check_vma=False,
    )
```

```python
import functools

import jax
import jax.numpy as jnp
from jax import lax
from jax.experimental import pallas as pl
from jax.experimental.pallas import tpu as pltpu
from jax.sharding import PartitionSpec as P

PARTS = 2
VMEM = pl.BlockSpec(memory_space=pltpu.VMEM)
SMEM = pl.BlockSpec(memory_space=pltpu.SMEM)
ANY = pl.BlockSpec(memory_space=pl.ANY)


def call(kernel, out_shape, in_specs, operands, flops=0):
    outs = out_shape if isinstance(out_shape, tuple) else (out_shape,)
    moved = sum(x.size * x.dtype.itemsize for x in (*operands, *outs))
    return pl.pallas_call(
        kernel,
        out_shape=out_shape,
        in_specs=in_specs,
        out_specs=jax.tree.map(lambda _: VMEM, out_shape),
        cost_estimate=pl.CostEstimate(flops=flops, bytes_accessed=moved, transcendentals=0),
        compiler_params=pltpu.CompilerParams(vmem_limit_bytes=32 * 1024 * 1024),
    )(*operands)


def split(value):
    high = value.astype(jnp.bfloat16)
    low = (value - high.astype(jnp.float32)).astype(jnp.bfloat16)
    return high, low


def dot(left, right):
    return jnp.dot(left, right, preferred_element_type=jnp.float32)


def pick_kernel(group, part, owners, arrived, out):
    chunk = out.shape[1]
    for number in range(out.shape[0]):
        out[number] = arrived[owners[0, number] % group, part * chunk:(part + 1) * chunk, :]


def merge_kernel(group, owners, mine, other, *refs):
    out = refs[-1]
    half = lax.axis_index("row") // group
    for number in range(out.shape[0]):
        here = owners[0, number] // group == half

        @pl.when(here)
        def _():
            out[number] = mine[number]

        @pl.when(jnp.logical_not(here))
        def _():
            out[number] = other[number]


def right_kernel(offsets, *refs):
    rights, (right_high, right_low) = refs[:-2], refs[-2:]
    count = offsets.shape[0]
    width = right_high.shape[0] // count
    blocks = rights[0].shape[0] // width
    for number in range(count):
        lanes = slice(number * width, (number + 1) * width)
        for step, ref in enumerate(rights):
            for block in range(blocks):

                @pl.when(offsets[number] == step * blocks + block)
                def _():
                    high, low = split(ref[block * width:(block + 1) * width, :])
                    right_high[lanes, :] = high
                    right_low[lanes, :] = low


def multiply_kernel(part, right_high, right_low, previous, *refs):
    group = len(refs) - part - 3
    pieces, early = refs[:group], refs[group:group + part]
    out, left_high, left_low = refs[group + part:]
    count, chunk, width = pieces[0].shape
    member = lax.axis_index("row") % group
    for number in range(count):
        lanes = slice(number * width, (number + 1) * width)
        for step in range(group):
            place = pl.multiple_of((member ^ step) * chunk, chunk)
            high, low = split(pieces[step][number])
            left_high[pl.ds(place, chunk), lanes] = high
            left_low[pl.ds(place, chunk), lanes] = low
    product = (
        dot(left_high[...], right_low[...])
        + dot(left_low[...], right_high[...])
        + dot(left_high[...], right_high[...])
    )
    if part < PARTS - 1:
        out[...] = product
    else:
        for number, ref in enumerate((*early, product)):
            for place in range(group):
                first = (place * PARTS + number) * chunk
                rows = slice(first, first + chunk)
                out[rows, :] = 2.0 * previous[rows, :] - ref[place * chunk:(place + 1) * chunk, :]


def shards(left_slots, right, previous, offsets, owners):
    own = left_slots[0]
    rows, width = own.shape
    count = offsets.shape[0]
    devices = lax.axis_size("row")
    columns = lax.axis_size("col")
    group = devices // 2
    size = rows // PARTS
    chunk = size // group
    piece = jax.ShapeDtypeStruct((count, chunk, width), own.dtype)

    def swap(array, mask):
        return lax.ppermute(array, "row", [(i, i ^ mask) for i in range(devices)])

    def shift(array, distance):
        pairs = [((i + distance) % columns, i) for i in range(columns)]
        return lax.ppermute(array, "col", pairs)

    groups = [list(range(first, first + group)) for first in range(0, devices, group)]
    arrived = lax.all_to_all(
        own.reshape(group, PARTS * chunk, width), "row", 0, 0, axis_index_groups=groups, tiled=True
    )
    mine = [
        call(functools.partial(pick_kernel, group, part), piece, [SMEM, VMEM], (owners, arrived))
        for part in range(PARTS)
    ]

    rights = [right] + [shift(right, distance) for distance in range(1, columns)]
    terms = jax.ShapeDtypeStruct((count * width, right.shape[1]), jnp.bfloat16)
    right_terms = call(
        right_kernel, (terms, terms), [SMEM] + [VMEM] * columns, (offsets, *rights), flops=4 * terms.size
    )

    results = []
    for part in range(PARTS):
        wait = right_terms[:1] if part == PARTS - 1 else ()
        merged = call(
            functools.partial(merge_kernel, group),
            piece,
            [SMEM, VMEM, VMEM] + [ANY] * len(wait),
            (owners, mine[part], swap(mine[part], group), *wait),
        )
        pieces = {0: merged}
        bits = [1 << b for b in range(1, group.bit_length() - 1)]
        for bit in bits if part % 2 else reversed(bits):
            for s in list(pieces):
                pieces[s + bit] = swap(pieces[s], bit)
        for s in list(pieces):
            pieces[s + 1] = swap(pieces[s], 1)
        last = part == PARTS - 1
        operands = (*right_terms, previous, *[pieces[s] for s in range(group)], *results)
        out_shape = jax.ShapeDtypeStruct((rows if last else size, right.shape[1]), previous.dtype)
        moved = sum(x.size * x.dtype.itemsize for x in operands)
        results.append(pl.pallas_call(
            functools.partial(multiply_kernel, part),
            out_shape=out_shape,
            in_specs=[VMEM] * len(operands),
            out_specs=VMEM,
            scratch_shapes=[pltpu.VMEM((size, count * width), jnp.bfloat16)] * 2,
            cost_estimate=pl.CostEstimate(
                flops=6 * size * count * width * right.shape[1], bytes_accessed=moved, transcendentals=0
            ),
            compiler_params=pltpu.CompilerParams(vmem_limit_bytes=32 * 1024 * 1024),
        )(*operands))
    return results[-1]


def solution(mesh):
    return jax.shard_map(
        shards,
        mesh=mesh,
        in_specs=(P("row", "col", None), P("col", "row"), P("col", "row"), P(), P("col", None)),
        out_specs=P("col", "row"),
        check_vma=False,
    )
```

```python
import functools

import jax
import jax.numpy as jnp
from jax import lax
from jax.experimental import pallas as pl
from jax.experimental.pallas import tpu as pltpu
from jax.sharding import PartitionSpec as P

PARTS = 2
VMEM = pl.BlockSpec(memory_space=pltpu.VMEM)
SMEM = pl.BlockSpec(memory_space=pltpu.SMEM)
ANY = pl.BlockSpec(memory_space=pl.ANY)


def call(kernel, out_shape, in_specs, operands, flops=0):
    outs = out_shape if isinstance(out_shape, tuple) else (out_shape,)
    moved = sum(x.size * x.dtype.itemsize for x in (*operands, *outs))
    return pl.pallas_call(
        kernel,
        out_shape=out_shape,
        in_specs=in_specs,
        out_specs=jax.tree.map(lambda _: VMEM, out_shape),
        cost_estimate=pl.CostEstimate(flops=flops, bytes_accessed=moved, transcendentals=0),
        compiler_params=pltpu.CompilerParams(vmem_limit_bytes=32 * 1024 * 1024),
    )(*operands)


def split(value):
    high = value.astype(jnp.bfloat16)
    low = (value - high.astype(jnp.float32)).astype(jnp.bfloat16)
    return high, low


def dot(left, right):
    return jnp.dot(left, right, preferred_element_type=jnp.float32)


def pick_kernel(group, owners, arrived, out):
    for number in range(out.shape[0]):
        out[number] = arrived[owners[0, number] % group]


def merge_kernel(group, owners, mine, other, *refs):
    out = refs[-1]
    half = lax.axis_index("row") // group
    for number in range(out.shape[0]):
        here = owners[0, number] // group == half

        @pl.when(here)
        def _():
            out[number] = mine[number]

        @pl.when(jnp.logical_not(here))
        def _():
            out[number] = other[number]


def right_kernel(offsets, *refs):
    rights, (right_high, right_low) = refs[:-2], refs[-2:]
    count = offsets.shape[0]
    width = right_high.shape[0] // count
    blocks = rights[0].shape[0] // width
    for number in range(count):
        lanes = slice(number * width, (number + 1) * width)
        for step, ref in enumerate(rights):
            for block in range(blocks):

                @pl.when(offsets[number] == step * blocks + block)
                def _():
                    high, low = split(ref[block * width:(block + 1) * width, :])
                    right_high[lanes, :] = high
                    right_low[lanes, :] = low


def multiply_kernel(part, right_high, right_low, previous, *refs):
    group = len(refs) - part - 3
    pieces, early = refs[:group], refs[group:group + part]
    out, left_high, left_low = refs[group + part:]
    count, chunk, width = pieces[0].shape
    member = lax.axis_index("row") % group
    for number in range(count):
        lanes = slice(number * width, (number + 1) * width)
        for step in range(group):
            place = pl.multiple_of((member ^ step) * chunk, chunk)
            high, low = split(pieces[step][number])
            left_high[pl.ds(place, chunk), lanes] = high
            left_low[pl.ds(place, chunk), lanes] = low
    product = (
        dot(left_high[...], right_low[...])
        + dot(left_low[...], right_high[...])
        + dot(left_high[...], right_high[...])
    )
    if part < PARTS - 1:
        out[...] = product
    else:
        size = group * chunk
        for number, ref in enumerate((*early, product)):
            rows = slice(number * size, (number + 1) * size)
            out[rows, :] = 2.0 * previous[rows, :] - ref[...]


def shards(left_slots, right, previous, offsets, owners):
    own = left_slots[0]
    rows, width = own.shape
    count = offsets.shape[0]
    devices = lax.axis_size("row")
    columns = lax.axis_size("col")
    group = devices // 2
    size = rows // PARTS
    chunk = size // group
    piece = jax.ShapeDtypeStruct((count, chunk, width), own.dtype)

    def swap(array, mask):
        return lax.ppermute(array, "row", [(i, i ^ mask) for i in range(devices)])

    def shift(array, distance):
        pairs = [((i + distance) % columns, i) for i in range(columns)]
        return lax.ppermute(array, "col", pairs)

    groups = [list(range(first, first + group)) for first in range(0, devices, group)]
    arrived = [
        lax.all_to_all(
            own[part * size:(part + 1) * size].reshape(group, chunk, width),
            "row", 0, 0, axis_index_groups=groups, tiled=True,
        )
        for part in range(PARTS)
    ]
    mine = [
        call(functools.partial(pick_kernel, group), piece, [SMEM, VMEM], (owners, array)) for array in arrived
    ]

    rights = [right] + [shift(right, distance) for distance in range(1, columns)]
    terms = jax.ShapeDtypeStruct((count * width, right.shape[1]), jnp.bfloat16)
    right_terms = call(
        right_kernel, (terms, terms), [SMEM] + [VMEM] * columns, (offsets, *rights), flops=4 * terms.size
    )

    results = []
    for part in range(PARTS):
        wait = right_terms[:1] if part == PARTS - 1 else ()
        merged = call(
            functools.partial(merge_kernel, group),
            piece,
            [SMEM, VMEM, VMEM] + [ANY] * len(wait),
            (owners, mine[part], swap(mine[part], group), *wait),
        )
        pieces = {0: merged}
        bits = [1 << b for b in range(1, group.bit_length() - 1)]
        for bit in bits if part % 2 else reversed(bits):
            for s in list(pieces):
                pieces[s + bit] = swap(pieces[s], bit)
        for s in list(pieces):
            pieces[s + 1] = swap(pieces[s], 1)
        last = part == PARTS - 1
        operands = (*right_terms, previous, *[pieces[s] for s in range(group)], *results)
        out_shape = jax.ShapeDtypeStruct((rows if last else size, right.shape[1]), previous.dtype)
        moved = sum(x.size * x.dtype.itemsize for x in operands)
        results.append(pl.pallas_call(
            functools.partial(multiply_kernel, part),
            out_shape=out_shape,
            in_specs=[VMEM] * len(operands),
            out_specs=VMEM,
            scratch_shapes=[pltpu.VMEM((size, count * width), jnp.bfloat16)] * 2,
            cost_estimate=pl.CostEstimate(
                flops=6 * size * count * width * right.shape[1], bytes_accessed=moved, transcendentals=0
            ),
            compiler_params=pltpu.CompilerParams(vmem_limit_bytes=32 * 1024 * 1024),
        )(*operands))
    return results[-1]


def solution(mesh):
    return jax.shard_map(
        shards,
        mesh=mesh,
        in_specs=(P("row", "col", None), P("col", "row"), P("col", "row"), P(), P("col", None)),
        out_specs=P("col", "row"),
        check_vma=False,
    )
```

```python
import functools

import jax
import jax.numpy as jnp
from jax import lax
from jax.experimental import pallas as pl
from jax.experimental.pallas import tpu as pltpu
from jax.sharding import PartitionSpec as P

PARTS = 2
VMEM = pl.BlockSpec(memory_space=pltpu.VMEM)
SMEM = pl.BlockSpec(memory_space=pltpu.SMEM)
ANY = pl.BlockSpec(memory_space=pl.ANY)


def call(kernel, out_shape, in_specs, operands, flops=0):
    outs = out_shape if isinstance(out_shape, tuple) else (out_shape,)
    moved = sum(x.size * x.dtype.itemsize for x in (*operands, *outs))
    return pl.pallas_call(
        kernel,
        out_shape=out_shape,
        in_specs=in_specs,
        out_specs=jax.tree.map(lambda _: VMEM, out_shape),
        cost_estimate=pl.CostEstimate(flops=flops, bytes_accessed=moved, transcendentals=0),
        compiler_params=pltpu.CompilerParams(vmem_limit_bytes=32 * 1024 * 1024),
    )(*operands)


def split(value):
    high = value.astype(jnp.bfloat16)
    low = (value - high.astype(jnp.float32)).astype(jnp.bfloat16)
    return high, low


def dot(left, right):
    return jnp.dot(left, right, preferred_element_type=jnp.float32)


def flag_kernel(group, few, owners, out):
    count = owners.shape[1]
    upper = jnp.int32(0)
    for number in range(count):
        upper += owners[0, number] // group
    many = jnp.where(jnp.maximum(upper, count - upper) > few, 1, 0)
    out[...] = jnp.full(out.shape, many, jnp.int32)


def copy_kernel(array, wait, out):
    out[...] = array[...]


def pick_kernel(group, owners, arrived, *outs):
    mine, packed, rest = outs[:PARTS], outs[PARTS:-1], outs[-1]
    count, chunk, _ = mine[0].shape
    few = packed[0].shape[0]
    half = lax.axis_index("row") // group
    before = jnp.int32(0)
    for number in range(count):
        owner = owners[0, number]
        member = owner % group
        here = owner // group == half
        for part in range(PARTS):
            rows = slice(part * chunk, (part + 1) * chunk)
            mine[part][number] = arrived[member, rows, :]
            for slot in range(number + 1):

                @pl.when(here & (before == slot))
                def _():
                    if slot < few:
                        packed[part][slot] = arrived[member, rows, :]
                    else:
                        rest[part, slot - few] = arrived[member, rows, :]

        before = jnp.where(here, before + 1, before)


def merge_kernel(group, part, owners, mine, other, rest, *refs):
    out = refs[-1]
    few = other.shape[0]
    half = lax.axis_index("row") // group
    before = jnp.int32(0)
    for number in range(out.shape[0]):
        here = owners[0, number] // group == half

        @pl.when(here)
        def _():
            out[number] = mine[number]

        for slot in range(number + 1):

            @pl.when(jnp.logical_not(here) & (before == slot))
            def _():
                out[number] = other[slot] if slot < few else rest[part, slot - few]

        before = jnp.where(here, before, before + 1)


def right_kernel(offsets, *refs):
    sources, (right_high, right_low) = refs[:-2], refs[-2:]
    count = offsets.shape[0]
    width = right_high.shape[0] // count
    blocks = [ref.at[place:place + width] for ref in sources for place in range(0, ref.shape[0], width)]
    for number in range(count):
        lanes = slice(number * width, (number + 1) * width)
        for block, ref in enumerate(blocks):

            @pl.when(offsets[number] == block)
            def _():
                high, low = split(ref[...])
                right_high[lanes, :] = high
                right_low[lanes, :] = low


def multiply_kernel(part, right_high, right_low, previous, *refs):
    group = len(refs) - part - 3
    pieces, early = refs[:group], refs[group:group + part]
    out, left_high, left_low = refs[group + part:]
    count, chunk, width = pieces[0].shape
    member = lax.axis_index("row") % group
    for number in range(count):
        lanes = slice(number * width, (number + 1) * width)
        for step in range(group):
            place = pl.multiple_of((member ^ step) * chunk, chunk)
            high, low = split(pieces[step][number])
            left_high[pl.ds(place, chunk), lanes] = high
            left_low[pl.ds(place, chunk), lanes] = low
    product = (
        dot(left_high[...], right_low[...])
        + dot(left_low[...], right_high[...])
        + dot(left_high[...], right_high[...])
    )
    if part < PARTS - 1:
        out[...] = product
    else:
        for number, ref in enumerate((*early, product)):
            for place in range(group):
                first = (place * PARTS + number) * chunk
                rows = slice(first, first + chunk)
                out[rows, :] = 2.0 * previous[rows, :] - ref[place * chunk:(place + 1) * chunk, :]


def shards(left_slots, right, previous, offsets, owners):
    own = left_slots[0]
    rows, width = own.shape
    count = offsets.shape[0]
    devices = lax.axis_size("row")
    columns = lax.axis_size("col")
    group = devices // 2
    size = rows // PARTS
    chunk = size // group
    piece = jax.ShapeDtypeStruct((count, chunk, width), own.dtype)

    def swap(array, mask):
        return lax.ppermute(array, "row", [(i, i ^ mask) for i in range(devices)])

    def shift(array, distance):
        pairs = [((i + distance) % columns, i) for i in range(columns)]
        return lax.ppermute(array, "col", pairs)

    groups = [list(range(first, first + group)) for first in range(0, devices, group)]
    arrived = lax.all_to_all(
        own.reshape(group, PARTS * chunk, width), "row", 0, 0, axis_index_groups=groups, tiled=True
    )
    few = (2 * count + 2) // 3
    packed = jax.ShapeDtypeStruct((few, chunk, width), own.dtype)
    extra = jax.ShapeDtypeStruct((PARTS, count - few, chunk, width), own.dtype)
    picked = call(
        functools.partial(pick_kernel, group),
        (piece,) * PARTS + (packed,) * PARTS + (extra,),
        [SMEM, VMEM],
        (owners, arrived),
    )
    mine, sent = picked[:PARTS], picked[PARTS:-1]
    others = [swap(array, group) for array in sent]

    flags = call(
        functools.partial(flag_kernel, group, few),
        jax.ShapeDtypeStruct((8, 128), jnp.int32),
        [SMEM],
        (owners,),
    )
    distance = 1
    while distance < columns:
        flags = flags | shift(flags, distance)
        distance *= 2
    rest = lax.cond(flags[0, 0] == 0, lambda array: array, lambda array: swap(array, group), picked[-1])

    given = call(copy_kernel, jax.ShapeDtypeStruct(right.shape, right.dtype), [VMEM, ANY], (right, flags))
    sources = [right] + [shift(given, distance) for distance in range(1, columns)]
    terms = jax.ShapeDtypeStruct((count * width, right.shape[1]), jnp.bfloat16)
    right_terms = call(
        right_kernel, (terms, terms), [SMEM] + [VMEM] * len(sources), (offsets, *sources), flops=4 * terms.size
    )

    results = []
    for part in range(PARTS):
        wait = right_terms[:1] if part == PARTS - 1 else ()
        merged = call(
            functools.partial(merge_kernel, group, part),
            piece,
            [SMEM, VMEM, VMEM, VMEM] + [ANY] * len(wait),
            (owners, mine[part], others[part], rest, *wait),
        )
        pieces = {0: merged}
        bits = [1 << b for b in range(1, group.bit_length() - 1)]
        for bit in bits if part % 2 else reversed(bits):
            for s in list(pieces):
                pieces[s + bit] = swap(pieces[s], bit)
        for s in list(pieces):
            pieces[s + 1] = swap(pieces[s], 1)
        last = part == PARTS - 1
        operands = (*right_terms, previous, *[pieces[s] for s in range(group)], *results)
        out_shape = jax.ShapeDtypeStruct((rows if last else size, right.shape[1]), previous.dtype)
        moved = sum(x.size * x.dtype.itemsize for x in operands)
        results.append(pl.pallas_call(
            functools.partial(multiply_kernel, part),
            out_shape=out_shape,
            in_specs=[VMEM] * len(operands),
            out_specs=VMEM,
            scratch_shapes=[pltpu.VMEM((size, count * width), jnp.bfloat16)] * 2,
            cost_estimate=pl.CostEstimate(
                flops=6 * size * count * width * right.shape[1], bytes_accessed=moved, transcendentals=0
            ),
            compiler_params=pltpu.CompilerParams(vmem_limit_bytes=32 * 1024 * 1024),
        )(*operands))
    return results[-1]


def solution(mesh):
    return jax.shard_map(
        shards,
        mesh=mesh,
        in_specs=(P("row", "col", None), P("col", "row"), P("col", "row"), P(), P("col", None)),
        out_specs=P("col", "row"),
        check_vma=False,
    )
```

```python
import functools

import jax
import jax.numpy as jnp
from jax import lax
from jax.experimental import pallas as pl
from jax.experimental.pallas import tpu as pltpu
from jax.sharding import PartitionSpec as P

PARTS = 2
VMEM = pl.BlockSpec(memory_space=pltpu.VMEM)
SMEM = pl.BlockSpec(memory_space=pltpu.SMEM)
ANY = pl.BlockSpec(memory_space=pl.ANY)


def call(kernel, out_shape, in_specs, operands, flops=0):
    outs = out_shape if isinstance(out_shape, tuple) else (out_shape,)
    moved = sum(x.size * x.dtype.itemsize for x in (*operands, *outs))
    return pl.pallas_call(
        kernel,
        out_shape=out_shape,
        in_specs=in_specs,
        out_specs=jax.tree.map(lambda _: VMEM, out_shape),
        cost_estimate=pl.CostEstimate(flops=flops, bytes_accessed=moved, transcendentals=0),
        compiler_params=pltpu.CompilerParams(vmem_limit_bytes=32 * 1024 * 1024),
    )(*operands)


def split(value):
    high = value.astype(jnp.bfloat16)
    low = (value - high.astype(jnp.float32)).astype(jnp.bfloat16)
    return high, low


def dot(left, right):
    return jnp.dot(left, right, preferred_element_type=jnp.float32)


def flag_kernel(group, few, owners, out):
    count = owners.shape[1]
    upper = jnp.int32(0)
    for number in range(count):
        upper += owners[0, number] // group
    many = jnp.where(jnp.maximum(upper, count - upper) > few, 1, 0)
    out[...] = jnp.full(out.shape, many, jnp.int32)


def copy_kernel(array, wait, out):
    out[...] = array[...]


def pick_kernel(group, owners, arrived, *outs):
    packed, rest = outs[:-1], outs[-1]
    few, chunk, _ = packed[0].shape
    half = lax.axis_index("row") // group
    before = jnp.int32(0)
    for number in range(owners.shape[1]):
        owner = owners[0, number]
        member = owner % group
        here = owner // group == half
        for slot in range(number + 1):

            @pl.when(here & (before == slot))
            def _():
                for part, ref in enumerate(packed):
                    rows = slice(part * chunk, (part + 1) * chunk)
                    if slot < few:
                        ref[slot] = arrived[member, rows, :]
                    else:
                        rest[part, slot - few] = arrived[member, rows, :]

        before = jnp.where(here, before + 1, before)


def merge_kernel(group, part, owners, arrived, other, rest, out):
    few, chunk, _ = other.shape
    half = lax.axis_index("row") // group
    before = jnp.int32(0)
    for number in range(out.shape[0]):
        owner = owners[0, number]
        here = owner // group == half

        @pl.when(here)
        def _():
            out[number] = arrived[owner % group, part * chunk:(part + 1) * chunk, :]

        for slot in range(number + 1):

            @pl.when(jnp.logical_not(here) & (before == slot))
            def _():
                out[number] = other[slot] if slot < few else rest[part, slot - few]

        before = jnp.where(here, before, before + 1)


def right_kernel(offsets, *refs):
    sources, (right_high, right_low) = refs[:-2], refs[-2:]
    count = offsets.shape[0]
    width = right_high.shape[0] // count
    blocks = [ref.at[place:place + width] for ref in sources for place in range(0, ref.shape[0], width)]
    for number in range(count):
        lanes = slice(number * width, (number + 1) * width)
        for block, ref in enumerate(blocks):

            @pl.when(offsets[number] == block)
            def _():
                high, low = split(ref[...])
                right_high[lanes, :] = high
                right_low[lanes, :] = low


def multiply_kernel(part, right_high, right_low, previous, *refs):
    group = len(refs) - part - 3
    pieces, early = refs[:group], refs[group:group + part]
    out, left_high, left_low = refs[group + part:]
    count, chunk, width = pieces[0].shape
    member = lax.axis_index("row") % group
    for number in range(count):
        lanes = slice(number * width, (number + 1) * width)
        for step in range(group):
            place = pl.multiple_of((member ^ step) * chunk, chunk)
            high, low = split(pieces[step][number])
            left_high[pl.ds(place, chunk), lanes] = high
            left_low[pl.ds(place, chunk), lanes] = low
    product = (
        dot(left_high[...], right_low[...])
        + dot(left_low[...], right_high[...])
        + dot(left_high[...], right_high[...])
    )
    if part < PARTS - 1:
        out[...] = product
    else:
        for number, ref in enumerate((*early, product)):
            for place in range(group):
                first = (place * PARTS + number) * chunk
                rows = slice(first, first + chunk)
                out[rows, :] = 2.0 * previous[rows, :] - ref[place * chunk:(place + 1) * chunk, :]


def shards(left_slots, right, previous, offsets, owners):
    own = left_slots[0]
    rows, width = own.shape
    count = offsets.shape[0]
    devices = lax.axis_size("row")
    columns = lax.axis_size("col")
    group = devices // 2
    size = rows // PARTS
    chunk = size // group
    piece = jax.ShapeDtypeStruct((count, chunk, width), own.dtype)

    def swap(array, mask):
        return lax.ppermute(array, "row", [(i, i ^ mask) for i in range(devices)])

    def shift(array, distance):
        pairs = [((i + distance) % columns, i) for i in range(columns)]
        return lax.ppermute(array, "col", pairs)

    groups = [list(range(first, first + group)) for first in range(0, devices, group)]
    arrived = lax.all_to_all(
        own.reshape(group, PARTS * chunk, width), "row", 0, 0, axis_index_groups=groups, tiled=True
    )
    few = (2 * count + 2) // 3
    packed = jax.ShapeDtypeStruct((few, chunk, width), own.dtype)
    extra = jax.ShapeDtypeStruct((PARTS, count - few, chunk, width), own.dtype)
    picked = call(
        functools.partial(pick_kernel, group),
        (packed,) * PARTS + (extra,),
        [SMEM, VMEM],
        (owners, arrived),
    )
    others = [swap(array, group) for array in picked[:-1]]

    flags = call(
        functools.partial(flag_kernel, group, few),
        jax.ShapeDtypeStruct((8, 128), jnp.int32),
        [SMEM],
        (owners,),
    )
    distance = 1
    while distance < columns:
        flags = flags | shift(flags, distance)
        distance *= 2
    rest = lax.cond(flags[0, 0] == 0, lambda array: array, lambda array: swap(array, group), picked[-1])

    given = call(copy_kernel, jax.ShapeDtypeStruct(right.shape, right.dtype), [VMEM, ANY], (right, flags))
    sources = [right] + [shift(given, distance) for distance in range(1, columns)]
    terms = jax.ShapeDtypeStruct((count * width, right.shape[1]), jnp.bfloat16)
    right_terms = call(
        right_kernel, (terms, terms), [SMEM] + [VMEM] * len(sources), (offsets, *sources), flops=4 * terms.size
    )

    results = []
    for part in range(PARTS):
        merged = call(
            functools.partial(merge_kernel, group, part),
            piece,
            [SMEM, VMEM, VMEM, VMEM],
            (owners, arrived, others[part], rest),
        )
        pieces = {0: merged}
        bits = [1 << b for b in range(1, group.bit_length() - 1)]
        for bit in bits if part % 2 else reversed(bits):
            for s in list(pieces):
                pieces[s + bit] = swap(pieces[s], bit)
        for s in list(pieces):
            pieces[s + 1] = swap(pieces[s], 1)
        last = part == PARTS - 1
        operands = (*right_terms, previous, *[pieces[s] for s in range(group)], *results)
        out_shape = jax.ShapeDtypeStruct((rows if last else size, right.shape[1]), previous.dtype)
        moved = sum(x.size * x.dtype.itemsize for x in operands)
        results.append(pl.pallas_call(
            functools.partial(multiply_kernel, part),
            out_shape=out_shape,
            in_specs=[VMEM] * len(operands),
            out_specs=VMEM,
            scratch_shapes=[pltpu.VMEM((size, count * width), jnp.bfloat16)] * 2,
            cost_estimate=pl.CostEstimate(
                flops=6 * size * count * width * right.shape[1], bytes_accessed=moved, transcendentals=0
            ),
            compiler_params=pltpu.CompilerParams(vmem_limit_bytes=32 * 1024 * 1024),
        )(*operands))
    return results[-1]


def solution(mesh):
    return jax.shard_map(
        shards,
        mesh=mesh,
        in_specs=(P("row", "col", None), P("col", "row"), P("col", "row"), P(), P("col", None)),
        out_specs=P("col", "row"),
        check_vma=False,
    )
```

```python
import functools

import jax
import jax.numpy as jnp
from jax import lax
from jax.experimental import pallas as pl
from jax.experimental.pallas import tpu as pltpu
from jax.sharding import PartitionSpec as P

PARTS = 2
VMEM = pl.BlockSpec(memory_space=pltpu.VMEM)
SMEM = pl.BlockSpec(memory_space=pltpu.SMEM)
ANY = pl.BlockSpec(memory_space=pl.ANY)


def call(kernel, out_shape, in_specs, operands, flops=0):
    outs = out_shape if isinstance(out_shape, tuple) else (out_shape,)
    moved = sum(x.size * x.dtype.itemsize for x in (*operands, *outs))
    return pl.pallas_call(
        kernel,
        out_shape=out_shape,
        in_specs=in_specs,
        out_specs=jax.tree.map(lambda _: VMEM, out_shape),
        cost_estimate=pl.CostEstimate(flops=flops, bytes_accessed=moved, transcendentals=0),
        compiler_params=pltpu.CompilerParams(vmem_limit_bytes=32 * 1024 * 1024),
    )(*operands)


def split(value):
    high = value.astype(jnp.bfloat16)
    low = (value - high.astype(jnp.float32)).astype(jnp.bfloat16)
    return high, low


def dot(left, right):
    return jnp.dot(left, right, preferred_element_type=jnp.float32)


def flag_kernel(group, few, owners, out):
    count = owners.shape[1]
    upper = jnp.int32(0)
    for number in range(count):
        upper += owners[0, number] // group
    many = jnp.where(jnp.maximum(upper, count - upper) > few, 1, 0)
    out[...] = jnp.full(out.shape, many, jnp.int32)


def copy_kernel(array, wait, out):
    out[...] = array[...]


def pick_kernel(group, owners, arrived, *outs):
    mine, packed, rest = outs[:PARTS], outs[PARTS:-1], outs[-1]
    count, chunk, _ = mine[0].shape
    few = packed[0].shape[0]
    half = lax.axis_index("row") // group
    before = jnp.int32(0)
    for number in range(count):
        owner = owners[0, number]
        member = owner % group
        here = owner // group == half
        for part in range(PARTS):
            rows = slice(part * chunk, (part + 1) * chunk)
            mine[part][number] = arrived[member, rows, :]
            for slot in range(number + 1):

                @pl.when(here & (before == slot))
                def _():
                    if slot < few:
                        packed[part][slot] = arrived[member, rows, :]
                    else:
                        rest[part, slot - few] = arrived[member, rows, :]

        before = jnp.where(here, before + 1, before)


def merge_kernel(group, part, owners, mine, other, rest, *refs):
    out = refs[-1]
    few = other.shape[0]
    half = lax.axis_index("row") // group
    before = jnp.int32(0)
    for number in range(out.shape[0]):
        here = owners[0, number] // group == half

        @pl.when(here)
        def _():
            out[number] = mine[number]

        for slot in range(number + 1):

            @pl.when(jnp.logical_not(here) & (before == slot))
            def _():
                out[number] = other[slot] if slot < few else rest[part, slot - few]

        before = jnp.where(here, before, before + 1)


def right_kernel(offsets, *refs):
    sources, (right_high, right_low) = refs[:-2], refs[-2:]
    count = offsets.shape[0]
    width = right_high.shape[0] // count
    blocks = [ref.at[place:place + width] for ref in sources for place in range(0, ref.shape[0], width)]
    for number in range(count):
        lanes = slice(number * width, (number + 1) * width)
        for block, ref in enumerate(blocks):

            @pl.when(offsets[number] == block)
            def _():
                high, low = split(ref[...])
                right_high[lanes, :] = high
                right_low[lanes, :] = low


def multiply_kernel(part, right_high, right_low, previous, *refs):
    group = len(refs) - part - 3
    pieces, early = refs[:group], refs[group:group + part]
    out, left_high, left_low = refs[group + part:]
    count, chunk, width = pieces[0].shape
    member = lax.axis_index("row") % group
    for number in range(count):
        lanes = slice(number * width, (number + 1) * width)
        for step in range(group):
            place = pl.multiple_of((member ^ step) * chunk, chunk)
            high, low = split(pieces[step][number])
            left_high[pl.ds(place, chunk), lanes] = high
            left_low[pl.ds(place, chunk), lanes] = low
    product = (
        dot(left_high[...], right_low[...])
        + dot(left_low[...], right_high[...])
        + dot(left_high[...], right_high[...])
    )
    if part < PARTS - 1:
        out[...] = product
    else:
        for number, ref in enumerate((*early, product)):
            for place in range(group):
                first = (place * PARTS + number) * chunk
                rows = slice(first, first + chunk)
                out[rows, :] = 2.0 * previous[rows, :] - ref[place * chunk:(place + 1) * chunk, :]


def shards(left_slots, right, previous, offsets, owners):
    own = left_slots[0]
    rows, width = own.shape
    count = offsets.shape[0]
    devices = lax.axis_size("row")
    columns = lax.axis_size("col")
    group = devices // 2
    size = rows // PARTS
    chunk = size // group
    piece = jax.ShapeDtypeStruct((count, chunk, width), own.dtype)

    def swap(array, mask):
        return lax.ppermute(array, "row", [(i, i ^ mask) for i in range(devices)])

    def shift(array, distance):
        pairs = [((i + distance) % columns, i) for i in range(columns)]
        return lax.ppermute(array, "col", pairs)

    groups = [list(range(first, first + group)) for first in range(0, devices, group)]
    arrived = lax.all_to_all(
        own.reshape(group, PARTS * chunk, width), "row", 0, 0, axis_index_groups=groups, tiled=True
    )
    few = (2 * count + 2) // 3
    packed = jax.ShapeDtypeStruct((few, chunk, width), own.dtype)
    extra = jax.ShapeDtypeStruct((PARTS, count - few, chunk, width), own.dtype)
    picked = call(
        functools.partial(pick_kernel, group),
        (piece,) * PARTS + (packed,) * PARTS + (extra,),
        [SMEM, VMEM],
        (owners, arrived),
    )
    mine, sent = picked[:PARTS], picked[PARTS:-1]
    others = [swap(array, group) for array in sent]

    flags = call(
        functools.partial(flag_kernel, group, few),
        jax.ShapeDtypeStruct((8, 128), jnp.int32),
        [SMEM],
        (owners,),
    )
    distance = 1
    while distance < columns:
        flags = flags | shift(flags, distance)
        distance *= 2
    rest = lax.cond(flags[0, 0] == 0, lambda array: array, lambda array: swap(array, group), picked[-1])

    place = right.shape[0] - width
    last, sources = right[place:], [right]
    if place:
        first = jax.ShapeDtypeStruct((place, right.shape[1]), right.dtype)
        first = call(copy_kernel, first, [VMEM, ANY], (right[:place], flags))
    for distance in range(1, columns):
        sources += [shift(first, distance)] if place else []
        sources.append(shift(last, distance))
    terms = jax.ShapeDtypeStruct((count * width, right.shape[1]), jnp.bfloat16)
    right_terms = call(
        right_kernel, (terms, terms), [SMEM] + [VMEM] * len(sources), (offsets, *sources), flops=4 * terms.size
    )

    results = []
    for part in range(PARTS):
        wait = right_terms[:1] if part == PARTS - 1 else ()
        merged = call(
            functools.partial(merge_kernel, group, part),
            piece,
            [SMEM, VMEM, VMEM, VMEM] + [ANY] * len(wait),
            (owners, mine[part], others[part], rest, *wait),
        )
        pieces = {0: merged}
        bits = [1 << b for b in range(1, group.bit_length() - 1)]
        for bit in bits if part % 2 else reversed(bits):
            for s in list(pieces):
                pieces[s + bit] = swap(pieces[s], bit)
        for s in list(pieces):
            pieces[s + 1] = swap(pieces[s], 1)
        last = part == PARTS - 1
        operands = (*right_terms, previous, *[pieces[s] for s in range(group)], *results)
        out_shape = jax.ShapeDtypeStruct((rows if last else size, right.shape[1]), previous.dtype)
        moved = sum(x.size * x.dtype.itemsize for x in operands)
        results.append(pl.pallas_call(
            functools.partial(multiply_kernel, part),
            out_shape=out_shape,
            in_specs=[VMEM] * len(operands),
            out_specs=VMEM,
            scratch_shapes=[pltpu.VMEM((size, count * width), jnp.bfloat16)] * 2,
            cost_estimate=pl.CostEstimate(
                flops=6 * size * count * width * right.shape[1], bytes_accessed=moved, transcendentals=0
            ),
            compiler_params=pltpu.CompilerParams(vmem_limit_bytes=32 * 1024 * 1024),
        )(*operands))
    return results[-1]


def solution(mesh):
    return jax.shard_map(
        shards,
        mesh=mesh,
        in_specs=(P("row", "col", None), P("col", "row"), P("col", "row"), P(), P("col", None)),
        out_specs=P("col", "row"),
        check_vma=False,
    )
```

```python
import functools

import jax
import jax.numpy as jnp
from jax import lax
from jax.experimental import pallas as pl
from jax.experimental.pallas import tpu as pltpu
from jax.sharding import PartitionSpec as P

PARTS = 2
VMEM = pl.BlockSpec(memory_space=pltpu.VMEM)
SMEM = pl.BlockSpec(memory_space=pltpu.SMEM)
ANY = pl.BlockSpec(memory_space=pl.ANY)


def call(kernel, out_shape, in_specs, operands, flops=0):
    outs = out_shape if isinstance(out_shape, tuple) else (out_shape,)
    moved = sum(x.size * x.dtype.itemsize for x in (*operands, *outs))
    return pl.pallas_call(
        kernel,
        out_shape=out_shape,
        in_specs=in_specs,
        out_specs=jax.tree.map(lambda _: VMEM, out_shape),
        cost_estimate=pl.CostEstimate(flops=flops, bytes_accessed=moved, transcendentals=0),
        compiler_params=pltpu.CompilerParams(vmem_limit_bytes=32 * 1024 * 1024),
    )(*operands)


def split(value):
    high = value.astype(jnp.bfloat16)
    low = (value - high.astype(jnp.float32)).astype(jnp.bfloat16)
    return high, low


def dot(left, right):
    return jnp.dot(left, right, preferred_element_type=jnp.float32)


def flag_kernel(group, few, owners, out):
    count = owners.shape[1]
    upper = jnp.int32(0)
    for number in range(count):
        upper += owners[0, number] // group
    many = jnp.where(jnp.maximum(upper, count - upper) > few, 1, 0)
    out[...] = jnp.full(out.shape, many, jnp.int32)


def copy_kernel(array, wait, out):
    out[...] = array[...]


def pick_kernel(group, owners, arrived, *outs):
    mine, packed, rest = outs[:PARTS], outs[PARTS:-1], outs[-1]
    count, chunk, _ = mine[0].shape
    few = packed[0].shape[0]
    half = lax.axis_index("row") // group
    members = [owners[0, number] % group for number in range(count)]
    slots = [members[0]] * count
    before = jnp.int32(0)
    for number in range(count):
        here = owners[0, number] // group == half
        slots = [jnp.where(here & (before == slot), members[number], old) for slot, old in enumerate(slots)]
        before = jnp.where(here, before + 1, before)
    for part in range(PARTS):
        rows = slice(part * chunk, (part + 1) * chunk)
        for slot in range(count):
            if slot < few:
                packed[part][slot] = arrived[slots[slot], rows, :]
            else:
                rest[part, slot - few] = arrived[slots[slot], rows, :]
            mine[part][slot] = arrived[members[slot], rows, :]


def merge_kernel(group, part, owners, mine, other, rest, *refs):
    out = refs[-1]
    few = other.shape[0]
    half = lax.axis_index("row") // group
    before = jnp.int32(0)
    for number in range(out.shape[0]):
        here = owners[0, number] // group == half

        @pl.when(here)
        def _():
            out[number] = mine[number]

        @pl.when(jnp.logical_not(here) & (before < few))
        def _():
            out[number] = other[jnp.minimum(before, few - 1)]

        @pl.when(jnp.logical_not(here) & (before >= few))
        def _():
            out[number] = rest[part, jnp.maximum(before - few, 0)]

        before = jnp.where(here, before, before + 1)


def right_kernel(offsets, *refs):
    sources, (right_high, right_low) = refs[:-2], refs[-2:]
    count = offsets.shape[0]
    width = right_high.shape[0] // count
    blocks = [ref.at[place:place + width] for ref in sources for place in range(0, ref.shape[0], width)]
    for number in range(count):
        lanes = slice(number * width, (number + 1) * width)
        for block, ref in enumerate(blocks):

            @pl.when(offsets[number] == block)
            def _():
                high, low = split(ref[...])
                right_high[lanes, :] = high
                right_low[lanes, :] = low


def multiply_kernel(part, right_high, right_low, previous, *refs):
    group = len(refs) - part - 3
    pieces, early = refs[:group], refs[group:group + part]
    out, left_high, left_low = refs[group + part:]
    count, chunk, width = pieces[0].shape
    member = lax.axis_index("row") % group
    for number in range(count):
        lanes = slice(number * width, (number + 1) * width)
        for step in range(group):
            place = pl.multiple_of((member ^ step) * chunk, chunk)
            high, low = split(pieces[step][number])
            left_high[pl.ds(place, chunk), lanes] = high
            left_low[pl.ds(place, chunk), lanes] = low
    product = (
        dot(left_high[...], right_low[...])
        + dot(left_low[...], right_high[...])
        + dot(left_high[...], right_high[...])
    )
    if part < PARTS - 1:
        out[...] = product
    else:
        for number, ref in enumerate((*early, product)):
            for place in range(group):
                first = (place * PARTS + number) * chunk
                rows = slice(first, first + chunk)
                out[rows, :] = 2.0 * previous[rows, :] - ref[place * chunk:(place + 1) * chunk, :]


def shards(left_slots, right, previous, offsets, owners):
    own = left_slots[0]
    rows, width = own.shape
    count = offsets.shape[0]
    devices = lax.axis_size("row")
    columns = lax.axis_size("col")
    group = devices // 2
    size = rows // PARTS
    chunk = size // group
    piece = jax.ShapeDtypeStruct((count, chunk, width), own.dtype)

    def swap(array, mask):
        return lax.ppermute(array, "row", [(i, i ^ mask) for i in range(devices)])

    def shift(array, distance):
        pairs = [((i + distance) % columns, i) for i in range(columns)]
        return lax.ppermute(array, "col", pairs)

    groups = [list(range(first, first + group)) for first in range(0, devices, group)]
    arrived = lax.all_to_all(
        own.reshape(group, PARTS * chunk, width), "row", 0, 0, axis_index_groups=groups, tiled=True
    )
    few = (2 * count + 2) // 3
    packed = jax.ShapeDtypeStruct((few, chunk, width), own.dtype)
    extra = jax.ShapeDtypeStruct((PARTS, count - few, chunk, width), own.dtype)
    picked = call(
        functools.partial(pick_kernel, group),
        (piece,) * PARTS + (packed,) * PARTS + (extra,),
        [SMEM, VMEM],
        (owners, arrived),
    )
    mine, sent = picked[:PARTS], picked[PARTS:-1]
    others = [swap(array, group) for array in sent]

    flags = call(
        functools.partial(flag_kernel, group, few),
        jax.ShapeDtypeStruct((8, 128), jnp.int32),
        [SMEM],
        (owners,),
    )
    distance = 1
    while distance < columns:
        flags = flags | shift(flags, distance)
        distance *= 2
    rest = lax.cond(flags[0, 0] == 0, lambda array: array, lambda array: swap(array, group), picked[-1])

    place = right.shape[0] - width
    last, sources = right[place:], [right]
    if place:
        first = jax.ShapeDtypeStruct((place, right.shape[1]), right.dtype)
        first = call(copy_kernel, first, [VMEM, ANY], (right[:place], flags))
    for distance in range(1, columns):
        sources += [shift(first, distance)] if place else []
        sources.append(shift(last, distance))
    terms = jax.ShapeDtypeStruct((count * width, right.shape[1]), jnp.bfloat16)
    right_terms = call(
        right_kernel, (terms, terms), [SMEM] + [VMEM] * len(sources), (offsets, *sources), flops=4 * terms.size
    )

    results = []
    for part in range(PARTS):
        wait = () if part else right_terms[:1]
        merged = call(
            functools.partial(merge_kernel, group, part),
            piece,
            [SMEM, VMEM, VMEM, VMEM] + [ANY] * len(wait),
            (owners, mine[part], others[part], rest, *wait),
        )
        pieces = {0: merged}
        bits = [1 << b for b in range(1, group.bit_length() - 1)]
        for bit in bits if part % 2 else reversed(bits):
            for s in list(pieces):
                pieces[s + bit] = swap(pieces[s], bit)
        for s in list(pieces):
            pieces[s + 1] = swap(pieces[s], 1)
        last = part == PARTS - 1
        operands = (*right_terms, previous, *[pieces[s] for s in range(group)], *results)
        out_shape = jax.ShapeDtypeStruct((rows if last else size, right.shape[1]), previous.dtype)
        moved = sum(x.size * x.dtype.itemsize for x in operands)
        results.append(pl.pallas_call(
            functools.partial(multiply_kernel, part),
            out_shape=out_shape,
            in_specs=[VMEM] * len(operands),
            out_specs=VMEM,
            scratch_shapes=[pltpu.VMEM((size, count * width), jnp.bfloat16)] * 2,
            cost_estimate=pl.CostEstimate(
                flops=6 * size * count * width * right.shape[1], bytes_accessed=moved, transcendentals=0
            ),
            compiler_params=pltpu.CompilerParams(vmem_limit_bytes=32 * 1024 * 1024),
        )(*operands))
    return results[-1]


def solution(mesh):
    return jax.shard_map(
        shards,
        mesh=mesh,
        in_specs=(P("row", "col", None), P("col", "row"), P("col", "row"), P(), P("col", None)),
        out_specs=P("col", "row"),
        check_vma=False,
    )
```

```python
import functools

import jax
import jax.numpy as jnp
from jax import lax
from jax.experimental import pallas as pl
from jax.experimental.pallas import tpu as pltpu
from jax.sharding import PartitionSpec as P

PARTS = 2
VMEM = pl.BlockSpec(memory_space=pltpu.VMEM)
SMEM = pl.BlockSpec(memory_space=pltpu.SMEM)
ANY = pl.BlockSpec(memory_space=pl.ANY)


def call(kernel, out_shape, in_specs, operands, flops=0):
    outs = out_shape if isinstance(out_shape, tuple) else (out_shape,)
    moved = sum(x.size * x.dtype.itemsize for x in (*operands, *outs))
    return pl.pallas_call(
        kernel,
        out_shape=out_shape,
        in_specs=in_specs,
        out_specs=jax.tree.map(lambda _: VMEM, out_shape),
        cost_estimate=pl.CostEstimate(flops=flops, bytes_accessed=moved, transcendentals=0),
        compiler_params=pltpu.CompilerParams(vmem_limit_bytes=16 * 1024 * 1024),
    )(*operands)


def split(value):
    high = value.astype(jnp.bfloat16)
    low = (value - high.astype(jnp.float32)).astype(jnp.bfloat16)
    return high, low


def dot(left, right):
    return jnp.dot(left, right, preferred_element_type=jnp.float32)


def flag_kernel(group, few, owners, out):
    count = owners.shape[1]
    upper = jnp.int32(0)
    for number in range(count):
        upper += owners[0, number] // group
    many = jnp.where(jnp.maximum(upper, count - upper) > few, 1, 0)
    out[...] = jnp.full(out.shape, many, jnp.int32)


def copy_kernel(array, wait, out):
    out[...] = array[...]


def pick_kernel(group, owners, arrived, *outs):
    mine, packed, rest = outs[:PARTS], outs[PARTS:-1], outs[-1]
    count, chunk, _ = mine[0].shape
    few = packed[0].shape[0]
    half = lax.axis_index("row") // group
    members = [owners[0, number] % group for number in range(count)]
    slots = [members[0]] * count
    before = jnp.int32(0)
    for number in range(count):
        here = owners[0, number] // group == half
        slots = [jnp.where(here & (before == slot), members[number], old) for slot, old in enumerate(slots)]
        before = jnp.where(here, before + 1, before)
    for part in range(PARTS):
        rows = slice(part * chunk, (part + 1) * chunk)
        for slot in range(count):
            if slot < few:
                packed[part][slot] = arrived[slots[slot], rows, :]
            else:
                rest[part, slot - few] = arrived[slots[slot], rows, :]
            mine[part][slot] = arrived[members[slot], rows, :]


def merge_kernel(group, part, owners, mine, other, rest, *refs):
    out = refs[-1]
    few = other.shape[0]
    half = lax.axis_index("row") // group
    before = jnp.int32(0)
    for number in range(out.shape[0]):
        here = owners[0, number] // group == half

        @pl.when(here)
        def _():
            out[number] = mine[number]

        @pl.when(jnp.logical_not(here) & (before < few))
        def _():
            out[number] = other[jnp.minimum(before, few - 1)]

        @pl.when(jnp.logical_not(here) & (before >= few))
        def _():
            out[number] = rest[part, jnp.maximum(before - few, 0)]

        before = jnp.where(here, before, before + 1)


def right_kernel(offsets, *refs):
    sources, (right_high, right_low) = refs[:-2], refs[-2:]
    count = offsets.shape[0]
    width = right_high.shape[0] // count
    blocks = [ref.at[place:place + width] for ref in sources for place in range(0, ref.shape[0], width)]
    for number in range(count):
        lanes = slice(number * width, (number + 1) * width)
        for block, ref in enumerate(blocks):

            @pl.when(offsets[number] == block)
            def _():
                high, low = split(ref[...])
                right_high[lanes, :] = high
                right_low[lanes, :] = low


def multiply_kernel(part, right_high, right_low, previous, *refs):
    group = len(refs) - part - 3
    pieces, early = refs[:group], refs[group:group + part]
    out, left_high, left_low = refs[group + part:]
    count, chunk, width = pieces[0].shape
    member = lax.axis_index("row") % group
    for number in range(count):
        lanes = slice(number * width, (number + 1) * width)
        for step in range(group):
            place = pl.multiple_of((member ^ step) * chunk, chunk)
            high, low = split(pieces[step][number])
            left_high[pl.ds(place, chunk), lanes] = high
            left_low[pl.ds(place, chunk), lanes] = low
    product = (
        dot(left_high[...], right_low[...])
        + dot(left_low[...], right_high[...])
        + dot(left_high[...], right_high[...])
    )
    if part < PARTS - 1:
        out[...] = product
    else:
        for number, ref in enumerate((*early, product)):
            for place in range(group):
                first = (place * PARTS + number) * chunk
                rows = slice(first, first + chunk)
                out[rows, :] = 2.0 * previous[rows, :] - ref[place * chunk:(place + 1) * chunk, :]


def shards(left_slots, right, previous, offsets, owners):
    own = left_slots[0]
    rows, width = own.shape
    count = offsets.shape[0]
    devices = lax.axis_size("row")
    columns = lax.axis_size("col")
    group = devices // 2
    size = rows // PARTS
    chunk = size // group
    piece = jax.ShapeDtypeStruct((count, chunk, width), own.dtype)

    def swap(array, mask):
        return lax.ppermute(array, "row", [(i, i ^ mask) for i in range(devices)])

    def shift(array, distance):
        pairs = [((i + distance) % columns, i) for i in range(columns)]
        return lax.ppermute(array, "col", pairs)

    groups = [list(range(first, first + group)) for first in range(0, devices, group)]
    arrived = lax.all_to_all(
        own.reshape(group, PARTS * chunk, width), "row", 0, 0, axis_index_groups=groups, tiled=True
    )
    few = (2 * count + 2) // 3
    packed = jax.ShapeDtypeStruct((few, chunk, width), own.dtype)
    extra = jax.ShapeDtypeStruct((PARTS, count - few, chunk, width), own.dtype)
    picked = call(
        functools.partial(pick_kernel, group),
        (piece,) * PARTS + (packed,) * PARTS + (extra,),
        [SMEM, VMEM],
        (owners, arrived),
    )
    mine, sent = picked[:PARTS], picked[PARTS:-1]
    others = [swap(array, group) for array in sent]

    flags = call(
        functools.partial(flag_kernel, group, few),
        jax.ShapeDtypeStruct((8, 128), jnp.int32),
        [SMEM],
        (owners,),
    )
    distance = 1
    while distance < columns:
        flags = flags | shift(flags, distance)
        distance *= 2
    rest = lax.cond(flags[0, 0] == 0, lambda array: array, lambda array: swap(array, group), picked[-1])

    place = right.shape[0] - width
    last, sources = right[place:], [right]
    if place:
        first = jax.ShapeDtypeStruct((place, right.shape[1]), right.dtype)
        first = call(copy_kernel, first, [VMEM, ANY], (right[:place], flags))
    for distance in range(1, columns):
        sources += [shift(first, distance)] if place else []
        sources.append(shift(last, distance))
    terms = jax.ShapeDtypeStruct((count * width, right.shape[1]), jnp.bfloat16)
    right_terms = call(
        right_kernel, (terms, terms), [SMEM] + [VMEM] * len(sources), (offsets, *sources), flops=4 * terms.size
    )

    results = []
    for part in range(PARTS):
        wait = right_terms[:1] if part == PARTS - 1 else ()
        merged = call(
            functools.partial(merge_kernel, group, part),
            piece,
            [SMEM, VMEM, VMEM, VMEM] + [ANY] * len(wait),
            (owners, mine[part], others[part], rest, *wait),
        )
        pieces = {0: merged}
        bits = [1 << b for b in range(1, group.bit_length() - 1)]
        for bit in bits if part % 2 else reversed(bits):
            for s in list(pieces):
                pieces[s + bit] = swap(pieces[s], bit)
        for s in list(pieces):
            pieces[s + 1] = swap(pieces[s], 1)
        last = part == PARTS - 1
        operands = (*right_terms, previous, *[pieces[s] for s in range(group)], *results)
        out_shape = jax.ShapeDtypeStruct((rows if last else size, right.shape[1]), previous.dtype)
        moved = sum(x.size * x.dtype.itemsize for x in operands)
        results.append(pl.pallas_call(
            functools.partial(multiply_kernel, part),
            out_shape=out_shape,
            in_specs=[VMEM] * len(operands),
            out_specs=VMEM,
            scratch_shapes=[pltpu.VMEM((size, count * width), jnp.bfloat16)] * 2,
            cost_estimate=pl.CostEstimate(
                flops=6 * size * count * width * right.shape[1], bytes_accessed=moved, transcendentals=0
            ),
            compiler_params=pltpu.CompilerParams(vmem_limit_bytes=16 * 1024 * 1024),
        )(*operands))
    return results[-1]


def solution(mesh):
    return jax.shard_map(
        shards,
        mesh=mesh,
        in_specs=(P("row", "col", None), P("col", "row"), P("col", "row"), P(), P("col", None)),
        out_specs=P("col", "row"),
        check_vma=False,
    )
```

```python
import functools

import jax
import jax.numpy as jnp
from jax import lax
from jax.experimental import pallas as pl
from jax.experimental.pallas import tpu as pltpu
from jax.sharding import PartitionSpec as P

PARTS = 2
VMEM = pl.BlockSpec(memory_space=pltpu.VMEM)
SMEM = pl.BlockSpec(memory_space=pltpu.SMEM)
ANY = pl.BlockSpec(memory_space=pl.ANY)


def call(kernel, out_shape, in_specs, operands, flops=0):
    outs = out_shape if isinstance(out_shape, tuple) else (out_shape,)
    moved = sum(x.size * x.dtype.itemsize for x in (*operands, *outs))
    return pl.pallas_call(
        kernel,
        out_shape=out_shape,
        in_specs=in_specs,
        out_specs=jax.tree.map(lambda _: VMEM, out_shape),
        cost_estimate=pl.CostEstimate(flops=flops, bytes_accessed=moved, transcendentals=0),
        compiler_params=pltpu.CompilerParams(vmem_limit_bytes=16 * 1024 * 1024),
    )(*operands)


def split(value):
    high = value.astype(jnp.bfloat16)
    low = (value - high.astype(jnp.float32)).astype(jnp.bfloat16)
    return high, low


def dot(left, right):
    return jnp.dot(left, right, preferred_element_type=jnp.float32)


def flag_kernel(group, few, owners, out):
    count = owners.shape[1]
    upper = jnp.int32(0)
    for number in range(count):
        upper += owners[0, number] // group
    many = jnp.where(jnp.maximum(upper, count - upper) > few, 1, 0)
    out[...] = jnp.full(out.shape, many, jnp.int32)


def copy_kernel(array, wait, out):
    out[...] = array[...]


def pick_kernel(group, owners, arrived, *outs):
    mine, packed, rest = outs[:PARTS], outs[PARTS:-1], outs[-1]
    count, chunk, _ = mine[0].shape
    few = packed[0].shape[0]
    half = lax.axis_index("row") // group
    members = [owners[0, number] % group for number in range(count)]
    slots = [members[0]] * count
    before = jnp.int32(0)
    for number in range(count):
        here = owners[0, number] // group == half
        slots = [jnp.where(here & (before == slot), members[number], old) for slot, old in enumerate(slots)]
        before = jnp.where(here, before + 1, before)
    for part in range(PARTS):
        rows = slice(part * chunk, (part + 1) * chunk)
        for slot in range(count):
            if slot < few:
                packed[part][slot] = arrived[slots[slot], rows, :]
            else:
                rest[part, slot - few] = arrived[slots[slot], rows, :]
            mine[part][slot] = arrived[members[slot], rows, :]


def merge_kernel(group, part, owners, mine, other, rest, *refs):
    out = refs[-1]
    few = other.shape[0]
    half = lax.axis_index("row") // group
    before = jnp.int32(0)
    for number in range(out.shape[0]):
        here = owners[0, number] // group == half

        @pl.when(here)
        def _():
            out[number] = mine[number]

        @pl.when(jnp.logical_not(here) & (before < few))
        def _():
            out[number] = other[jnp.minimum(before, few - 1)]

        @pl.when(jnp.logical_not(here) & (before >= few))
        def _():
            out[number] = rest[part, jnp.maximum(before - few, 0)]

        before = jnp.where(here, before, before + 1)


def right_kernel(offsets, *refs):
    sources, (right_high, right_low) = refs[:-2], refs[-2:]
    count = offsets.shape[0]
    width = right_high.shape[0] // count
    blocks = [ref.at[place:place + width] for ref in sources for place in range(0, ref.shape[0], width)]
    for number in range(count):
        lanes = slice(number * width, (number + 1) * width)
        for block, ref in enumerate(blocks):

            @pl.when(offsets[number] == block)
            def _():
                high, low = split(ref[...])
                right_high[lanes, :] = high
                right_low[lanes, :] = low


def multiply_kernel(part, right_high, right_low, previous, *refs):
    group = len(refs) - part - 3
    pieces, early = refs[:group], refs[group:group + part]
    out, left_high, left_low = refs[group + part:]
    count, chunk, width = pieces[0].shape
    member = lax.axis_index("row") % group
    for number in range(count):
        lanes = slice(number * width, (number + 1) * width)
        for step in range(group):
            place = pl.multiple_of((member ^ step) * chunk, chunk)
            high, low = split(pieces[step][number])
            left_high[pl.ds(place, chunk), lanes] = high
            left_low[pl.ds(place, chunk), lanes] = low
    product = (
        dot(left_high[...], right_low[...])
        + dot(left_low[...], right_high[...])
        + dot(left_high[...], right_high[...])
    )
    if part < PARTS - 1:
        out[...] = product
    else:
        for number, ref in enumerate((*early, product)):
            for place in range(group):
                first = (place * PARTS + number) * chunk
                rows = slice(first, first + chunk)
                out[rows, :] = 2.0 * previous[rows, :] - ref[place * chunk:(place + 1) * chunk, :]


def shards(left_slots, right, previous, offsets, owners):
    own = left_slots[0]
    rows, width = own.shape
    count = offsets.shape[0]
    devices = lax.axis_size("row")
    columns = lax.axis_size("col")
    group = devices // 2
    size = rows // PARTS
    chunk = size // group
    piece = jax.ShapeDtypeStruct((count, chunk, width), own.dtype)

    def swap(array, mask):
        return lax.ppermute(array, "row", [(i, i ^ mask) for i in range(devices)])

    def shift(array, distance):
        pairs = [((i + distance) % columns, i) for i in range(columns)]
        return lax.ppermute(array, "col", pairs)

    groups = [list(range(first, first + group)) for first in range(0, devices, group)]
    arrived = lax.all_to_all(
        own.reshape(group, PARTS * chunk, width), "row", 0, 0, axis_index_groups=groups, tiled=True
    )
    few = (2 * count + 2) // 3
    packed = jax.ShapeDtypeStruct((few, chunk, width), own.dtype)
    extra = jax.ShapeDtypeStruct((PARTS, count - few, chunk, width), own.dtype)
    picked = call(
        functools.partial(pick_kernel, group),
        (piece,) * PARTS + (packed,) * PARTS + (extra,),
        [SMEM, VMEM],
        (owners, arrived),
    )
    mine, sent = picked[:PARTS], picked[PARTS:-1]
    others = [swap(array, group) for array in sent]

    flags = call(
        functools.partial(flag_kernel, group, few),
        jax.ShapeDtypeStruct((8, 128), jnp.int32),
        [SMEM],
        (owners,),
    )
    distance = 1
    while distance < columns:
        flags = flags | shift(flags, distance)
        distance *= 2
    rest = lax.cond(flags[0, 0] == 0, lambda array: array, lambda array: swap(array, group), picked[-1])

    place = right.shape[0] - width
    last, sources = right[place:], [right]
    if place:
        first = jax.ShapeDtypeStruct((place, right.shape[1]), right.dtype)
        first = call(copy_kernel, first, [VMEM, ANY], (right[:place], flags))
    for distance in range(1, columns):
        sources += [shift(first, distance)] if place else []
        sources.append(shift(last, distance))
    terms = jax.ShapeDtypeStruct((count * width, right.shape[1]), jnp.bfloat16)
    right_terms = call(
        right_kernel, (terms, terms), [SMEM] + [VMEM] * len(sources), (offsets, *sources), flops=4 * terms.size
    )

    results = []
    for part in range(PARTS):
        wait = right_terms[:1] if part == PARTS - 1 else ()
        merged = call(
            functools.partial(merge_kernel, group, part),
            piece,
            [SMEM, VMEM, VMEM, VMEM] + [ANY] * len(wait),
            (owners, mine[part], others[part], rest, *wait),
        )
        pieces = {0: merged}
        bits = [1 << b for b in range(1, group.bit_length() - 1)]
        for bit in reversed(bits) if part % 2 else bits:
            for s in list(pieces):
                pieces[s + bit] = swap(pieces[s], bit)
        for s in list(pieces):
            pieces[s + 1] = swap(pieces[s], 1)
        last = part == PARTS - 1
        operands = (*right_terms, previous, *[pieces[s] for s in range(group)], *results)
        out_shape = jax.ShapeDtypeStruct((rows if last else size, right.shape[1]), previous.dtype)
        moved = sum(x.size * x.dtype.itemsize for x in operands)
        results.append(pl.pallas_call(
            functools.partial(multiply_kernel, part),
            out_shape=out_shape,
            in_specs=[VMEM] * len(operands),
            out_specs=VMEM,
            scratch_shapes=[pltpu.VMEM((size, count * width), jnp.bfloat16)] * 2,
            cost_estimate=pl.CostEstimate(
                flops=6 * size * count * width * right.shape[1], bytes_accessed=moved, transcendentals=0
            ),
            compiler_params=pltpu.CompilerParams(vmem_limit_bytes=16 * 1024 * 1024),
        )(*operands))
    return results[-1]


def solution(mesh):
    return jax.shard_map(
        shards,
        mesh=mesh,
        in_specs=(P("row", "col", None), P("col", "row"), P("col", "row"), P(), P("col", None)),
        out_specs=P("col", "row"),
        check_vma=False,
    )
```

```python
import functools

import jax
import jax.numpy as jnp
from jax import lax
from jax.experimental import pallas as pl
from jax.experimental.pallas import tpu as pltpu
from jax.sharding import PartitionSpec as P

PARTS = 2
VMEM = pl.BlockSpec(memory_space=pltpu.VMEM)
SMEM = pl.BlockSpec(memory_space=pltpu.SMEM)
ANY = pl.BlockSpec(memory_space=pl.ANY)


def call(kernel, out_shape, in_specs, operands, flops=0):
    outs = out_shape if isinstance(out_shape, tuple) else (out_shape,)
    moved = sum(x.size * x.dtype.itemsize for x in (*operands, *outs))
    return pl.pallas_call(
        kernel,
        out_shape=out_shape,
        in_specs=in_specs,
        out_specs=jax.tree.map(lambda _: VMEM, out_shape),
        cost_estimate=pl.CostEstimate(flops=flops, bytes_accessed=moved, transcendentals=0),
        compiler_params=pltpu.CompilerParams(vmem_limit_bytes=16 * 1024 * 1024),
    )(*operands)


def split(value):
    high = value.astype(jnp.bfloat16)
    low = (value - high.astype(jnp.float32)).astype(jnp.bfloat16)
    return high, low


def dot(left, right):
    return jnp.dot(left, right, preferred_element_type=jnp.float32)


def flag_kernel(group, few, owners, out):
    count = owners.shape[1]
    upper = jnp.int32(0)
    for number in range(count):
        upper += owners[0, number] // group
    many = jnp.where(jnp.maximum(upper, count - upper) > few, 1, 0)
    out[...] = jnp.full(out.shape, many, jnp.int32)


def copy_kernel(array, wait, out):
    out[...] = array[...]


def pick_kernel(group, owners, arrived, *outs):
    first = outs[0]
    few, chunk, _ = first.shape
    count = owners.shape[1]
    half = lax.axis_index("row") // group
    members = [owners[0, number] % group for number in range(count)]
    slots = [members[0]] * count
    before = jnp.int32(0)
    for number in range(count):
        here = owners[0, number] // group == half
        slots = [jnp.where(here & (before == slot), members[number], old) for slot, old in enumerate(slots)]
        before = jnp.where(here, before + 1, before)
    if len(outs) == 1:
        for slot in range(few):
            first[slot] = arrived[slots[slot], :chunk, :]
        return
    packed, mine, rest = outs[:PARTS - 1], outs[PARTS - 1:-1], outs[-1]
    for part in range(PARTS):
        rows = slice(part * chunk, (part + 1) * chunk)
        for slot in range(count):
            if slot >= few:
                rest[part, slot - few] = arrived[slots[slot], rows, :]
            elif part:
                packed[part - 1][slot] = arrived[slots[slot], rows, :]
            mine[part][slot] = arrived[members[slot], rows, :]


def merge_kernel(group, part, owners, mine, other, rest, *refs):
    out = refs[-1]
    few = other.shape[0]
    half = lax.axis_index("row") // group
    before = jnp.int32(0)
    for number in range(out.shape[0]):
        here = owners[0, number] // group == half

        @pl.when(here)
        def _():
            out[number] = mine[number]

        @pl.when(jnp.logical_not(here) & (before < few))
        def _():
            out[number] = other[jnp.minimum(before, few - 1)]

        @pl.when(jnp.logical_not(here) & (before >= few))
        def _():
            out[number] = rest[part, jnp.maximum(before - few, 0)]

        before = jnp.where(here, before, before + 1)


def right_kernel(offsets, wait, *refs):
    sources, (right_high, right_low) = refs[:-2], refs[-2:]
    count = offsets.shape[0]
    width = right_high.shape[0] // count
    blocks = [ref.at[place:place + width] for ref in sources for place in range(0, ref.shape[0], width)]
    for number in range(count):
        lanes = slice(number * width, (number + 1) * width)
        for block, ref in enumerate(blocks):

            @pl.when(offsets[number] == block)
            def _():
                high, low = split(ref[...])
                right_high[lanes, :] = high
                right_low[lanes, :] = low


def multiply_kernel(part, right_high, right_low, previous, *refs):
    group = len(refs) - part - 3
    pieces, early = refs[:group], refs[group:group + part]
    out, left_high, left_low = refs[group + part:]
    count, chunk, width = pieces[0].shape
    member = lax.axis_index("row") % group
    for number in range(count):
        lanes = slice(number * width, (number + 1) * width)
        for step in range(group):
            place = pl.multiple_of((member ^ step) * chunk, chunk)
            high, low = split(pieces[step][number])
            left_high[pl.ds(place, chunk), lanes] = high
            left_low[pl.ds(place, chunk), lanes] = low
    product = (
        dot(left_high[...], right_low[...])
        + dot(left_low[...], right_high[...])
        + dot(left_high[...], right_high[...])
    )
    if part < PARTS - 1:
        out[...] = product
    else:
        for number, ref in enumerate((*early, product)):
            for place in range(group):
                first = (place * PARTS + number) * chunk
                rows = slice(first, first + chunk)
                out[rows, :] = 2.0 * previous[rows, :] - ref[place * chunk:(place + 1) * chunk, :]


def shards(left_slots, right, previous, offsets, owners):
    own = left_slots[0]
    rows, width = own.shape
    count = offsets.shape[0]
    devices = lax.axis_size("row")
    columns = lax.axis_size("col")
    group = devices // 2
    size = rows // PARTS
    chunk = size // group
    piece = jax.ShapeDtypeStruct((count, chunk, width), own.dtype)

    def swap(array, mask):
        return lax.ppermute(array, "row", [(i, i ^ mask) for i in range(devices)])

    def shift(array, distance):
        pairs = [((i + distance) % columns, i) for i in range(columns)]
        return lax.ppermute(array, "col", pairs)

    groups = [list(range(first, first + group)) for first in range(0, devices, group)]
    arrived = lax.all_to_all(
        own.reshape(group, PARTS * chunk, width), "row", 0, 0, axis_index_groups=groups, tiled=True
    )
    few = (2 * count + 2) // 3
    packed = jax.ShapeDtypeStruct((few, chunk, width), own.dtype)
    extra = jax.ShapeDtypeStruct((PARTS, count - few, chunk, width), own.dtype)
    start = call(functools.partial(pick_kernel, group), packed, [SMEM, VMEM], (owners, arrived))
    picked = call(
        functools.partial(pick_kernel, group),
        (packed,) * (PARTS - 1) + (piece,) * PARTS + (extra,),
        [SMEM, VMEM],
        (owners, arrived),
    )
    sent, mine = (start, *picked[:PARTS - 1]), picked[PARTS - 1:-1]
    others = [swap(array, group) for array in sent]

    flags = call(
        functools.partial(flag_kernel, group, few),
        jax.ShapeDtypeStruct((8, 128), jnp.int32),
        [SMEM],
        (owners,),
    )
    distance = 1
    while distance < columns:
        flags = flags | shift(flags, distance)
        distance *= 2
    rest = lax.cond(flags[0, 0] == 0, lambda array: array, lambda array: swap(array, group), picked[-1])

    place = right.shape[0] - width
    last, sources = right[place:], [right]
    if place:
        first = jax.ShapeDtypeStruct((place, right.shape[1]), right.dtype)
        first = call(copy_kernel, first, [VMEM, ANY], (right[:place], flags))
    for distance in range(1, columns):
        sources += [shift(first, distance)] if place else []
        sources.append(shift(last, distance))
    terms = jax.ShapeDtypeStruct((count * width, right.shape[1]), jnp.bfloat16)
    results = []
    for part in range(PARTS):
        wait = right_terms[:1] if part else ()
        merged = call(
            functools.partial(merge_kernel, group, part),
            piece,
            [SMEM, VMEM, VMEM, VMEM] + [ANY] * len(wait),
            (owners, mine[part], others[part], rest, *wait),
        )
        pieces = {0: merged}
        bits = [1 << b for b in range(1, group.bit_length() - 1)]
        for bit in bits if part % 2 else reversed(bits):
            for s in list(pieces):
                pieces[s + bit] = swap(pieces[s], bit)
        for s in list(pieces):
            pieces[s + 1] = swap(pieces[s], 1)
        if part == 0:
            right_terms = call(
                right_kernel,
                (terms, terms),
                [SMEM, ANY] + [VMEM] * len(sources),
                (offsets, pieces[1], *sources),
                flops=4 * terms.size,
            )
        last = part == PARTS - 1
        operands = (*right_terms, previous, *[pieces[s] for s in range(group)], *results)
        out_shape = jax.ShapeDtypeStruct((rows if last else size, right.shape[1]), previous.dtype)
        moved = sum(x.size * x.dtype.itemsize for x in operands)
        results.append(pl.pallas_call(
            functools.partial(multiply_kernel, part),
            out_shape=out_shape,
            in_specs=[VMEM] * len(operands),
            out_specs=VMEM,
            scratch_shapes=[pltpu.VMEM((size, count * width), jnp.bfloat16)] * 2,
            cost_estimate=pl.CostEstimate(
                flops=6 * size * count * width * right.shape[1], bytes_accessed=moved, transcendentals=0
            ),
            compiler_params=pltpu.CompilerParams(vmem_limit_bytes=16 * 1024 * 1024),
        )(*operands))
    return results[-1]


def solution(mesh):
    return jax.shard_map(
        shards,
        mesh=mesh,
        in_specs=(P("row", "col", None), P("col", "row"), P("col", "row"), P(), P("col", None)),
        out_specs=P("col", "row"),
        check_vma=False,
    )
```
